256 devices in a mesh: dp: 8 (over x, core), graph: 32 (over z, y).
Axes of the slice: x: 4, y: 4, z: 8, core: 2. Of those that a mesh axis runs over, the one named last changes fastest.
Arguments:
- node_feats: bfloat16 [8, 512, 3712], P('dp', 'graph'), may hold values from -6 to 6
- node_cotan: bfloat16 [8, 512, 3712], P('dp', 'graph'), may hold values from -6 to 6
- source: int32 [8, 10240], P('dp', 'graph'), may hold values from 0 to 511, as said below
- target: int32 [8, 10240], P('dp', 'graph'), may hold values from 0 to 511, as said below
- angle: float32 [8, 10240], P('dp', 'graph'), may hold values from -3.140625 to 3.140625
- w_zero: bfloat16 [896, 896], replicated, may hold values from -0.1875 to 0.1875
- w_one: bfloat16 [768, 1536], replicated, may hold values from -0.21875 to 0.21875
- w_two: bfloat16 [640, 1280], replicated, may hold values from -0.25 to 0.25
Outputs:
- grad_nodes: bfloat16 [8, 512, 3712], P('dp', 'graph')
- grad_zero: float32 [896, 896], P('graph')
- grad_one: float32 [768, 1536], P('graph')
- grad_two: float32 [640, 1280], P('graph')
The draws below stay inside these ranges and needn't reach their ends.
Inputs may be any that keep to these rules, and one draw needn't show every extreme that they name: `source`: the edges at positions d * 320 to (d + 1) * 320 - 1 of a batch have both ends among atoms d * 16 - 8 to (d + 1) * 16 + 7; the first and the last of these atoms that lie in the batch are named on every device; no edge joins an atom to itself. `target`: as for source, with the same ranges per device.
All inputs are finite; a program needn't handle non-finite values.
Results may differ from the reference program's by a relative error of at most 0.0015.
The reference program's roundings to bfloat16 on the way count: a program that leaves them out, or rounds other values in their place, can miss the bound.
Values may be sent and summed in bfloat16 or wider, within the bound.
A program may use at most 128 MiB of HBM per device.

```python
import jax
import jax.numpy as jnp
from jax import lax

C = 128
HEADS = 8
ATOM_DEV = 16
EDGE_DEV = 320
REACH = 8
ATOMS = 512
EDGES = 10240
GROUPS = 8


def edge_pair(key):
    folded = jax.random.fold_in(key, 4242)
    first_key, second_key = jax.random.split(folded)
    position = jnp.arange(EDGES, dtype=jnp.int32)
    device = position // EDGE_DEV
    within = position % EDGE_DEV
    lower = jnp.maximum(device * ATOM_DEV - REACH, 0)
    upper = jnp.minimum((device + 1) * ATOM_DEV + REACH, ATOMS)
    extent = upper - lower
    target = lower + jax.random.randint(first_key, (GROUPS, EDGES), 0, 1 << 24, dtype=jnp.int32) % extent
    offset = jax.random.randint(second_key, (GROUPS, EDGES), 0, 1 << 24, dtype=jnp.int32) % (extent - 1)
    source = lower + offset
    source = jnp.where(source >= target, source + 1, source)
    source = jnp.where(within == 0, lower, source)
    target = jnp.where(within == 0, upper - 1, target)
    source = jnp.where(within == 1, upper - 1, source)
    target = jnp.where(within == 1, lower, target)
    return (source.astype(jnp.int32), target.astype(jnp.int32))


def draw_source(key, part):
    return edge_pair(key)[0]


def draw_target(key, part):
    return edge_pair(key)[1]


def block_levels(rng, shape, shards, low, largest):
    factor_of = 1.0
    for axis_at, parts in shards:
        heights = jax.random.uniform(jax.random.fold_in(jax.random.fold_in(rng, 6), axis_at), (parts,), jnp.float32, low / len(shards), largest / len(shards))
        factor_of = factor_of * jnp.repeat(jnp.exp(heights), shape[axis_at] // parts).reshape((-1,) + (1,) * (len(shape) - 1 - axis_at))
    return factor_of


def centred(stream_key, shape, scale, limit, shards=(), kind=jnp.bfloat16):
    factor_of = block_levels(stream_key, shape, shards, -0.22, 0.18) if shards else 1.0
    values = jax.random.normal(stream_key, shape, jnp.float32) * scale * factor_of
    return jnp.minimum(jnp.maximum(values, -limit), limit).astype(kind)


def setup_inputs(seed: int = 0) -> dict:
    key_of = jax.random.split(jax.random.key(seed), 9)
    return {
        "node_feats": centred(key_of[0], (GROUPS, ATOMS, 29 * C), 1.0, 6.0, ((0, 8), (1, 32))),
        "node_cotan": centred(key_of[1], (GROUPS, ATOMS, 29 * C), 1.0, 6.0, ((0, 8), (1, 32))),
        "source": draw_source(jax.random.fold_in(key_of[8], 71), 0),
        "target": draw_target(jax.random.fold_in(key_of[8], 71), 0),
        "angle": jnp.clip(jax.random.uniform(key_of[4], (GROUPS, EDGES), jnp.float32, -3.140625, 3.140625), -3.140625, 3.140625),
        "w_zero": centred(key_of[5], (7 * C, 7 * C), (7 * C) ** -0.5, 0.1875),
        "w_one": centred(key_of[6], (6 * C, 12 * C), (6 * C) ** -0.5, 0.21875),
        "w_two": centred(key_of[7], (5 * C, 10 * C), (5 * C) ** -0.5, 0.25),
    }


def contract_rows(first, second):
    return lax.dot_general(first, second, (((0,), (0,)), ((), ())), preferred_element_type=jnp.float32)

def contract_cols(first, weight):
    return lax.dot_general(first, weight, (((1,), (1,)), ((), ())), preferred_element_type=jnp.float32)

def rotate(first, second, cosine, sine):
    return (cosine * first - sine * second, sine * first + cosine * second)

def per_head(block, channels, heads):
    count = block.shape[0]
    return block.reshape(count, -1, heads, channels // heads)

def edge_terms(feats, cotan, phases, w_zero, w_one, w_two, channels, heads):
    count = feats.shape[0]
    bounds = [0, 7 * channels, 13 * channels, 19 * channels, 24 * channels, 29 * channels]
    cos_one = jnp.cos(phases)[:, None]
    sin_one = jnp.sin(phases)[:, None]
    cos_two = jnp.cos(2.0 * phases)[:, None]
    sin_two = jnp.sin(2.0 * phases)[:, None]
    zero_in = feats[:, :bounds[1]]
    pieces = [feats[:, bounds[k]:bounds[k + 1]].astype(jnp.float32) for k in range(1, 5)]
    rot_p1, rot_n1 = rotate(pieces[0], pieces[1], cos_one, sin_one)
    rot_p2, rot_n2 = rotate(pieces[2], pieces[3], cos_two, sin_two)
    stack_one = jnp.concatenate([rot_p1.astype(jnp.bfloat16), rot_n1.astype(jnp.bfloat16)], 0)
    stack_two = jnp.concatenate([rot_p2.astype(jnp.bfloat16), rot_n2.astype(jnp.bfloat16)], 0)
    zero_out = jnp.dot(zero_in, w_zero, preferred_element_type=jnp.float32)
    prod_one = jnp.dot(stack_one, w_one, preferred_element_type=jnp.float32)
    prod_two = jnp.dot(stack_two, w_two, preferred_element_type=jnp.float32)
    half_one = 6 * channels
    half_two = 5 * channels
    out_p1 = prod_one[:count, :half_one] - prod_one[count:, half_one:]
    out_n1 = prod_one[:count, half_one:] + prod_one[count:, :half_one]
    out_p2 = prod_two[:count, :half_two] - prod_two[count:, half_two:]
    out_n2 = prod_two[:count, half_two:] + prod_two[count:, :half_two]
    scale = 1.0 / jnp.sqrt(jnp.float32(channels // heads))
    logits = per_head(zero_out[:, :channels], channels, heads).sum(axis=(1, 3)) * scale
    gate = jax.nn.sigmoid(logits)
    grads_in = [cotan[:, bounds[k]:bounds[k + 1]].astype(jnp.float32) for k in range(5)]
    du_zero = grads_in[0]
    du_p1, du_n1 = rotate(grads_in[1], grads_in[2], cos_one, sin_one)
    du_p2, du_n2 = rotate(grads_in[3], grads_in[4], cos_two, sin_two)
    dgate = jnp.zeros((count, heads), jnp.float32)
    for upstream, forward in ((du_zero, zero_out), (du_p1, out_p1), (du_n1, out_n1), (du_p2, out_p2), (du_n2, out_n2)):
        dgate = dgate + per_head(upstream * forward, channels, heads).sum(axis=(1, 3))
    dlogit = dgate * gate * (1.0 - gate) * scale

    def gated(block):
        shaped = per_head(block, channels, heads) * gate[:, None, :, None]
        return shaped.reshape(count, -1)
    dz_zero = gated(du_zero)
    dz_zero = jnp.concatenate([dz_zero[:, :channels] + jnp.repeat(dlogit, channels // heads, axis=1), dz_zero[:, channels:]], 1)
    dz_zero = dz_zero.astype(jnp.bfloat16)
    dz_p1, dz_n1, dz_p2, dz_n2 = (gated(du_p1), gated(du_n1), gated(du_p2), gated(du_n2))
    grad_one = jnp.concatenate([jnp.concatenate([dz_p1, dz_n1], 1), jnp.concatenate([dz_n1, -dz_p1], 1)], 0).astype(jnp.bfloat16)
    grad_two = jnp.concatenate([jnp.concatenate([dz_p2, dz_n2], 1), jnp.concatenate([dz_n2, -dz_p2], 1)], 0).astype(jnp.bfloat16)
    back_zero = contract_cols(dz_zero, w_zero)
    back_one = contract_cols(grad_one, w_one)
    back_two = contract_cols(grad_two, w_two)
    dp_one, dn_one = rotate(back_one[:count], back_one[count:], cos_one, -sin_one)
    dp_two, dn_two = rotate(back_two[:count], back_two[count:], cos_two, -sin_two)
    node_terms = jnp.concatenate([back_zero, dp_one, dn_one, dp_two, dn_two], 1)
    return (node_terms, contract_rows(zero_in, dz_zero), contract_rows(stack_one, grad_one), contract_rows(stack_two, grad_two))

def reference(node_feats, node_cotan, source, target, angle, w_zero, w_one, w_two):
    channels = w_zero.shape[0] // 7
    blocks = EDGES // EDGE_DEV
    width = node_feats.shape[2]

    def one_group(items):
        feats, cotan, sources, targets, phases = items

        def advance(carry, block):
            grads, acc_zero, acc_one, acc_two = carry
            src_rows, dst_rows, block_phases = block
            node_terms, part_zero, part_one, part_two = edge_terms(feats[src_rows], cotan[dst_rows], block_phases, w_zero, w_one, w_two, channels, HEADS)
            return ((grads.at[src_rows].add(node_terms), acc_zero + part_zero, acc_one + part_one, acc_two + part_two), None)
        start = (jnp.zeros((ATOMS, width), jnp.float32), jnp.zeros(w_zero.shape, jnp.float32), jnp.zeros(w_one.shape, jnp.float32), jnp.zeros(w_two.shape, jnp.float32))
        blocked = (sources.reshape(blocks, EDGE_DEV).astype(jnp.int32), targets.reshape(blocks, EDGE_DEV).astype(jnp.int32), phases.reshape(blocks, EDGE_DEV))
        (grads, acc_zero, acc_one, acc_two), _ = lax.scan(advance, start, blocked)
        return (grads.astype(jnp.bfloat16), acc_zero, acc_one, acc_two)
    grads, acc_zero, acc_one, acc_two = lax.map(one_group, (node_feats, node_cotan, source, target, angle))
    return (grads, acc_zero.sum(0) / GROUPS, acc_one.sum(0) / GROUPS, acc_two.sum(0) / GROUPS)
```

```python
import functools

import jax
import jax.numpy as jnp
from jax import lax
from jax.experimental import pallas as pl
from jax.experimental.pallas import tpu as pltpu
from jax.sharding import PartitionSpec as P

MESH = pl.DeviceIdType.MESH
F32 = jnp.float32
BF16 = jnp.bfloat16
HEADS = 8
LANES = 128
EDGES = 320
PADDED = 384
BLOCKS = 29
ZERO, ONE, TWO = 7, 6, 5
AT_Z, AT_P1, AT_N1, AT_P2, AT_N2 = 0, 7, 13, 19, 24
VMEM_LIMIT = 62 * 1024 * 1024


def dot(a, b):
    return jnp.dot(a, b, preferred_element_type=F32)


def dot_t(a, b):
    return lax.dot_general(a, b, (((1,), (1,)), ((), ())), preferred_element_type=F32)


def dot_first(a, b):
    return lax.dot_general(a, b, (((0,), (0,)), ((), ())), preferred_element_type=F32)


def split2(v):
    high = v.astype(BF16)
    return high, (v - high.astype(F32)).astype(BF16)


def split3(v):
    high = v.astype(BF16)
    rest = v - high.astype(F32)
    middle = rest.astype(BF16)
    return high, middle, (rest - middle.astype(F32)).astype(BF16)


def chunks(count):
    out, at = [], 0
    while at < count:
        width = min(2, count - at)
        out.append((at, width))
        at += width
    return out


def cols(block, width=1):
    return pl.ds(block * LANES, width * LANES)


def wide(v, width):
    return v if width == 1 else jnp.concatenate([v] * width, axis=1)


def folded(v, width):
    return v if width == 1 else v[:, :LANES] + v[:, LANES:]


def edge_kernel(rows_ref, tab_ref, w0_ref, w1_ref, w2_ref, xt_ref, d_ref, node_ref, x_s, du_s, trig_s, oh_s):
    rows = rows_ref[...]
    parts = jnp.concatenate(list(split3(rows)), axis=0)
    pick_row = lax.broadcasted_iota(jnp.int32, (24, 6 * LANES), 0)
    pick_col = lax.broadcasted_iota(jnp.int32, (24, 6 * LANES), 1)
    chosen = jnp.where(pick_row % 8 == pick_col // LANES, 1.0, 0.0).astype(BF16)
    spread = dot_first(parts, chosen)
    for k in range(4):
        trig_s[k] = spread[:, k * LANES : (k + 1) * LANES]
    lane = lax.broadcasted_iota(jnp.int32, (EDGES, LANES), 1).astype(F32)
    for k in range(2):
        oh_s[k] = jnp.where(spread[:, (4 + k) * LANES : (5 + k) * LANES] == lane, 1.0, 0.0).astype(BF16)
    depth = tab_ref.shape[0]
    oh_src = oh_s[0, :, :depth]
    oh_dst = oh_s[1, :, :depth]

    xt_ref[:, :, EDGES:] = jnp.zeros((BLOCKS, LANES, PADDED - EDGES), BF16)
    d_ref[:, EDGES:, :] = jnp.zeros((BLOCKS, PADDED - EDGES, LANES), BF16)

    def keep_x(block, width, v):
        x_s[:, cols(block, width)] = v
        for w in range(width):
            xt_ref[block + w, :, :EDGES] = v[:, w * LANES : (w + 1) * LANES].T

    def rotated(onehot, c, s, plus, minus, width):
        a = dot(onehot, tab_ref[:, cols(plus, width)])
        b = dot(onehot, tab_ref[:, cols(minus, width)])
        return c * a - s * b, s * a + c * b

    for at, width in chunks(ZERO):
        keep_x(at, width, dot(oh_src, tab_ref[:, cols(at, width)]).astype(BF16))
    for m, (count, plus, minus) in enumerate(((ONE, AT_P1, AT_N1), (TWO, AT_P2, AT_N2))):
        for at, width in chunks(count):
            c, s = wide(trig_s[2 * m], width), wide(trig_s[2 * m + 1], width)
            p, n = rotated(oh_src, c, s, plus + at, minus + at, width)
            keep_x(plus + at, width, p.astype(BF16))
            keep_x(minus + at, width, n.astype(BF16))

    total = jnp.zeros((EDGES, LANES), F32)
    first = None
    for at, width in chunks(ZERO):
        out = dot(x_s[:, cols(0, ZERO)], w0_ref[:, cols(at, width)])
        if at == 0:
            first = out[:, :LANES]
        up = dot(oh_dst, tab_ref[:, cols(at, width)])
        du_s[:, cols(at, width)] = up
        total = total + folded(up * out, width)
    for m, (count, plus, minus, w_ref) in enumerate(((ONE, AT_P1, AT_N1, w1_ref), (TWO, AT_P2, AT_N2, w2_ref))):
        for at, width in chunks(count):
            c, s = wide(trig_s[2 * m], width), wide(trig_s[2 * m + 1], width)
            up_p, up_n = rotated(oh_dst, c, s, plus + at, minus + at, width)
            du_s[:, cols(plus + at, width)] = up_p
            du_s[:, cols(minus + at, width)] = up_n
            xp, xn = x_s[:, cols(plus, count)], x_s[:, cols(minus, count)]
            left, right = w_ref[:, cols(at, width)], w_ref[:, cols(count + at, width)]
            out_p = dot(xp, left) - dot(xn, right)
            out_n = dot(xp, right) + dot(xn, left)
            total = total + folded(up_p * out_p + up_n * out_n, width)

    size = LANES // HEADS
    head_r = lax.broadcasted_iota(jnp.int32, (LANES, LANES), 0) // size
    head_c = lax.broadcasted_iota(jnp.int32, (LANES, LANES), 1) // size
    same = jnp.where(head_r == head_c, 1.0, 0.0).astype(BF16)

    def head_sum(v):
        high, middle, low = split3(v)
        return dot(low, same) + dot(middle, same) + dot(high, same)

    scale = 1.0 / (float(size) ** 0.5)
    gate = jax.nn.sigmoid(head_sum(first) * scale)
    dlogit = head_sum(total) * gate * (1.0 - gate) * scale
    for block in range(BLOCKS):
        v = du_s[:, cols(block)] * gate
        if block == 0:
            v = v + dlogit
        d_ref[block, :EDGES, :] = v.astype(BF16)

    atoms = node_ref.shape[0]
    atom = lax.broadcasted_iota(jnp.int32, (atoms, EDGES), 0)
    table_row = jnp.where(atom < 8, atom + 32, jnp.where(atom < 16, atom - 8, jnp.where(atom < 24, atom, atom + 24)))
    oh_rows = jnp.where(table_row.astype(F32) == rows[4:5, :], 1.0, 0.0).astype(BF16)

    def scatter(block, width, v):
        high, low = split2(v)
        node_ref[:, cols(block, width)] = dot(oh_rows, high) + dot(oh_rows, low)

    def dconv(block, count):
        return jnp.concatenate([d_ref[block + k, :EDGES, :] for k in range(count)], axis=1)

    dz = dconv(AT_Z, ZERO)
    for at, width in chunks(ZERO):
        scatter(at, width, dot_t(dz, w0_ref[cols(at, width), :]))
    for m, (count, plus, minus, w_ref) in enumerate(((ONE, AT_P1, AT_N1, w1_ref), (TWO, AT_P2, AT_N2, w2_ref))):
        dp, dn = dconv(plus, count), dconv(minus, count)
        for at, width in chunks(count):
            c, s = wide(trig_s[2 * m], width), wide(trig_s[2 * m + 1], width)
            left, right = w_ref[cols(at, width), cols(0, count)], w_ref[cols(at, width), cols(count, count)]
            back_p = dot_t(dp, left) + dot_t(dn, right)
            back_n = dot_t(dn, left) - dot_t(dp, right)
            scatter(plus + at, width, c * back_p + s * back_n)
            scatter(minus + at, width, c * back_n - s * back_p)


def edge_call(rows, table, w_zero, w_one, w_two):
    width = table.shape[1]
    vmem = pl.BlockSpec(memory_space=pltpu.VMEM)
    return pl.pallas_call(
        edge_kernel,
        out_shape=(
            jax.ShapeDtypeStruct((BLOCKS, LANES, PADDED), BF16),
            jax.ShapeDtypeStruct((BLOCKS, PADDED, LANES), BF16),
            jax.ShapeDtypeStruct((32, width), F32),
        ),
        in_specs=[vmem] * 5,
        out_specs=(vmem,) * 3,
        scratch_shapes=[
            pltpu.VMEM((EDGES, width), BF16),
            pltpu.VMEM((EDGES, width), F32),
            pltpu.VMEM((4, EDGES, LANES), F32),
            pltpu.VMEM((2, EDGES, LANES), BF16),
        ],
        compiler_params=pltpu.CompilerParams(vmem_limit_bytes=VMEM_LIMIT),
        name="edge_terms",
    )(rows, table, w_zero, w_one, w_two)


SHARES = (
    ((0, 7, 29), (1, 7, 21), (1, 24, 26)),
    ((0, 0, 7), (0, 19, 29), (1, 0, 7), (1, 21, 24), (1, 26, 29)),
)
ONE_ORDER = tuple(b for j in range(3) for b in (2 * j, 2 * j + 1, 6 + 2 * j, 7 + 2 * j))
TILES = (
    tuple((1, i, b) for b in ONE_ORDER for i in range(3)) + tuple((2, i, b) for b in (0, 1, 5, 6) for i in range(3)),
    tuple((0, i, b) for b in range(7) for i in range(4)) + tuple((2, i, b) for b in (2, 3, 4, 7, 8, 9) for i in range(3)),
)
PLACE = tuple({tile: at for at, tile in enumerate(order)} for order in TILES)
NX, NY, NZ, NK = 4, 4, 8, 4
AXES = (("z", "x", "y"), ("x", "y", "z"), ("y", "z", "x"))
COUNT = {"x": NX, "y": NY, "z": NZ}


def chains_of(n):
    return ((1, 0, n // 2), (-1, 1, n // 2), (1, 1, n // 2 - 1), (-1, 0, n // 2 - 1))


def reduce_kernel(
    xt_ref, d_ref, node_ref,
    nodes_out, zero_out, one_out, two_out,
    xt_s, d_s, part0, part1, part2, r10, r11, r12, s20, s21, s22, r20, r21, r22, s30, s31, s32, r30, r31, r32,
    gathered, result, node_in,
    load_sem, share_send, share_recv, send1, recv1, send2, recv2, send3, recv3, all_send, all_recv, node_send, node_recv,
):
    dp = lax.axis_index("dp")
    graph = lax.axis_index("graph")
    core, x = dp % 2, dp // 2
    y, z = graph % NY, graph // NY
    place = {"x": x, "y": y, "z": z}

    def moved(axis, offset):
        n = COUNT[axis]
        to = (place[axis] + offset + n) % n
        if axis == "x":
            return {"dp": to * 2 + core, "graph": graph}
        if axis == "y":
            return {"dp": dp, "graph": z * NY + to}
        return {"dp": dp, "graph": to * NY + y}

    sibling = {"dp": x * 2 + (1 - core), "graph": graph}
    graphs = NY * NZ
    before = {"dp": dp, "graph": (graph + graphs - 1) % graphs}
    after = {"dp": dp, "graph": (graph + 1) % graphs}
    peers = [{"dp": (dp + o) % 8, "graph": graph} for o in range(1, 8)]
    peers += [moved("y", o) for o in range(1, NY)] + [moved("z", o) for o in range(1, NZ)] + [before, after]

    barrier = pltpu.get_barrier_semaphore()
    for peer in peers:
        pl.semaphore_signal(barrier, inc=1, device_id=peer, device_id_type=MESH)
    pl.semaphore_wait(barrier, len(peers))

    def remote(src, dst, send, recv, device):
        return pltpu.make_async_remote_copy(
            src_ref=src, dst_ref=dst, send_sem=send, recv_sem=recv, device_id=device, device_id_type=MESH
        )

    node_up = remote(node_ref.at[pl.ds(0, 8)], node_in.at[1], node_send.at[0], node_recv.at[0], before)
    node_down = remote(node_ref.at[pl.ds(24, 8)], node_in.at[0], node_send.at[1], node_recv.at[1], after)

    def own_half(kind, lo, hi, half):
        if kind == 0:
            return xt_s.at[pl.ds(lo, hi - lo), :, pl.ds(half * PADDED, PADDED)]
        return d_s.at[pl.ds(lo, hi - lo), pl.ds(half * PADDED, PADDED), :]

    def source_of(kind, lo, hi):
        return (d_ref if kind else xt_ref).at[pl.ds(lo, hi - lo)]

    def share_copy(k, span):
        return remote(source_of(*span), own_half(*span, 1), share_send.at[k], share_recv.at[k], sibling)

    def load_copy(k, span):
        return pltpu.make_async_copy(source_of(*span), own_half(*span, 0), load_sem.at[k])

    stage1 = (part0, part1, part2)
    rings1 = (r10, r11, r12)
    stage2 = (s20, s21, s22)
    rings2 = (r20, r21, r22)
    stage3 = (s30, s31, s32)
    slots3 = (r30, r31, r32)

    def slot_of(n, chain, step):
        return sum(c[2] for c in chains_of(n)[:chain]) + step

    def ring_copy(part, stage, chain, step):
        axis = AXES[part][stage]
        n = COUNT[axis]
        way, half, steps = chains_of(n)[chain]
        source, ring = ((stage1, rings1), (stage2, rings2))[stage]
        sends, recvs = ((send1, recv1), (send2, recv2))[stage]
        deep = source[part].shape[1] // 2
        slot = slot_of(n, chain, step)
        if step == 0:
            block = (place[axis] + way * steps + n) % n
            src = source[part].at[block, pl.ds(half * deep, deep)]
        else:
            src = ring[part].at[slot - 1]
        return remote(src, ring[part].at[slot], sends.at[part, slot], recvs.at[part, slot], moved(axis, way))

    def begin(part, stage):
        for chain in range(4):
            ring_copy(part, stage, chain, 0).start()

    def advance(part, stage, step):
        axis = AXES[part][stage]
        n = COUNT[axis]
        source, ring = ((stage1, rings1), (stage2, rings2))[stage]
        deep = source[part].shape[1] // 2
        for chain, (way, half, steps) in enumerate(chains_of(n)):
            if step < steps:
                slot = slot_of(n, chain, step)
                ring_copy(part, stage, chain, step - 1).wait_recv()
                block = (place[axis] + way * (steps - step) + n) % n
                ring[part][slot - 1] = ring[part][slot - 1] + source[part][block, pl.ds(half * deep, deep)]
                ring_copy(part, stage, chain, step).start()

    def finish(part, stage, out):
        axis = AXES[part][stage]
        n = COUNT[axis]
        source, ring = ((stage1, rings1), (stage2, rings2))[stage]
        deep = source[part].shape[1] // 2
        for half in range(2):
            arrived = []
            for chain, (way, h, steps) in enumerate(chains_of(n)):
                if h == half:
                    ring_copy(part, stage, chain, steps - 1).wait_recv()
                    arrived.append(ring[part][slot_of(n, chain, steps - 1)])
            out[pl.ds(half * deep, deep)] = source[part][place[axis], pl.ds(half * deep, deep)] + arrived[0] + arrived[1]

    def sent(part, stage):
        for chain, (way, half, steps) in enumerate(chains_of(COUNT[AXES[part][stage]])):
            for step in range(steps):
                ring_copy(part, stage, chain, step).wait_send()

    def last_copy(part, offset):
        axis = AXES[part][2]
        n = COUNT[axis]
        return remote(
            stage3[part].at[(place[axis] + offset) % n], slots3[part].at[offset - 1],
            send3.at[part, offset - 1], recv3.at[part, offset - 1], moved(axis, offset),
        )

    def put(which, tile, row_y, v):
        at = PLACE[which][tile]
        part, px, pk = at // 16, (at % 16) // 4, at % 4
        if part == 0:
            part0[:, px, row_y, pk] = v
        elif part == 1:
            part1[px, row_y, :, pk] = v
        else:
            part2[row_y, :, px, pk] = v

    def pair(block, width):
        return jnp.concatenate([d_s[block + k] for k in range(width)], axis=1)

    def factor(block, count):
        return xt_s[pl.ds(block, count)].reshape(count * LANES, 2 * PADDED)

    def put_aligned(v, first_blocks):
        shaped = v.reshape(NZ, NY * 3, 8, v.shape[1])
        for w, b in enumerate(first_blocks):
            for row_y in range(NY):
                for i in range(3):
                    put(0, (1, i, b), row_y, shaped[:, row_y * 3 + i, :, w * LANES : (w + 1) * LANES])

    def put_shifted(which, matrix, tiles, shard, v, first_blocks):
        result[:, pl.ds(0, NY * shard), pl.ds(0, v.shape[1])] = v.reshape(NZ, NY * shard, v.shape[1])
        for w, b in enumerate(first_blocks):
            for row_y in range(NY):
                for i in range(tiles):
                    put(which, (matrix, i, b), row_y, result[:, pl.ds(row_y * shard + i * 8, 8), cols(w)])

    def two_blocks(which, at, width):
        dp_, dn_ = pair(AT_P2 + at, width), pair(AT_N2 + at, width)
        rp, rn = factor(AT_P2, TWO), factor(AT_N2, TWO)
        put_shifted(which, 2, 3, 20, dot(rp, dp_) + dot(rn, dn_), range(at, at + width))
        put_shifted(which, 2, 3, 20, dot(rp, dn_) - dot(rn, dp_), range(TWO + at, TWO + at + width))

    node_up.start()
    node_down.start()
    result[...] = jnp.zeros_like(result)

    @pl.when(core == 0)
    def _():
        for k, span in enumerate(SHARES[1]):
            share_copy(k, span).start()
        for k, span in enumerate(SHARES[0]):
            load_copy(k, span).start()
        for k, span in enumerate(SHARES[0]):
            load_copy(k, span).wait()
            share_copy(k, span).wait_recv()
        for j in range(3):
            dp_, dn_ = pair(AT_P1 + 2 * j, 2), pair(AT_N1 + 2 * j, 2)
            rp, rn = factor(AT_P1, ONE), factor(AT_N1, ONE)
            put_aligned(dot(rp, dp_) + dot(rn, dn_), (2 * j, 2 * j + 1))
            put_aligned(dot(rp, dn_) - dot(rn, dp_), (6 + 2 * j, 7 + 2 * j))
            if j:
                begin(j - 1, 0)
        two_blocks(0, 0, 2)
        begin(2, 0)
        for k, span in enumerate(SHARES[1]):
            share_copy(k, span).wait_send()

    @pl.when(core == 1)
    def _():
        for k, span in enumerate(SHARES[0]):
            share_copy(k, span).start()
        for k, span in enumerate(SHARES[1]):
            load_copy(k, span).start()
        for k, span in enumerate(SHARES[1]):
            load_copy(k, span).wait()
            share_copy(k, span).wait_recv()
        blank = jnp.zeros((NZ, 8, LANES), F32)
        for row_y in range(NY):
            for k in (2, 3):
                part2[row_y, :, 3, k] = blank
        for at, width in chunks(ZERO):
            put_shifted(1, 0, 4, 28, dot(factor(AT_Z, ZERO), pair(AT_Z + at, width)), range(at, at + width))
            if at == 2:
                begin(0, 0)
        two_blocks(1, 2, 2)
        begin(1, 0)
        two_blocks(1, 4, 1)
        begin(2, 0)
        for k, span in enumerate(SHARES[0]):
            share_copy(k, span).wait_send()

    node_up.wait()
    node_down.wait()
    nodes_out[pl.ds(0, 8)] = (node_ref[pl.ds(8, 8)] + node_in[0]).astype(BF16)
    nodes_out[pl.ds(8, 8)] = (node_ref[pl.ds(16, 8)] + node_in[1]).astype(BF16)

    advance(1, 0, 1)
    advance(2, 0, 1)
    advance(0, 0, 1)
    advance(0, 0, 2)
    finish(1, 0, s21)
    begin(1, 1)
    finish(2, 0, s22)
    begin(2, 1)
    advance(0, 0, 3)
    advance(1, 1, 1)
    advance(2, 1, 1)
    finish(0, 0, s20)
    begin(0, 1)
    finish(1, 1, s31)
    for offset in range(1, NZ):
        last_copy(1, offset).start()
    advance(2, 1, 2)
    advance(0, 1, 1)
    advance(2, 1, 3)
    finish(0, 1, s30)
    for offset in range(1, NY):
        last_copy(0, offset).start()
    finish(2, 1, s32)
    for offset in range(1, NX):
        last_copy(2, offset).start()
    for part in range(3):
        axis = AXES[part][2]
        sum_ = stage3[part][place[axis]]
        for offset in range(1, COUNT[axis]):
            last_copy(part, offset).wait_recv()
            sum_ = sum_ + slots3[part][offset - 1]
        gathered[dp, pl.ds(part * NK, NK)] = sum_

    def all_copy(offset):
        return remote(
            gathered.at[dp], gathered.at[dp], all_send.at[offset - 1], all_recv.at[offset - 1],
            {"dp": (dp + offset) % 8, "graph": graph},
        )

    for offset in range(1, 8):
        all_copy(offset).start()
    for part in range(3):
        sent(part, 0)
        sent(part, 1)
        for offset in range(1, COUNT[AXES[part][2]]):
            last_copy(part, offset).wait_send()
    for offset in range(1, 8):
        all_copy(offset).wait_recv()
    outs = (zero_out, one_out, two_out)
    for which in range(2):
        for at, (matrix, i, b) in enumerate(TILES[which]):
            part, px, pk = at // 16, (at % 16) // 4, at % 4
            out = outs[matrix]
            rows = min(8, out.shape[0] - 8 * i)
            out[pl.ds(8 * i, rows), cols(b)] = gathered[px * 2 + which, part * NK + pk, pl.ds(0, rows)] * 0.125
    for offset in range(1, 8):
        all_copy(offset).wait_send()


def reduce_call(xt, d, node):
    width = node.shape[1]
    vmem = pl.BlockSpec(memory_space=pltpu.VMEM)
    hbm = pl.BlockSpec(memory_space=pl.ANY)
    tile = (NK, 8, LANES)
    dims = [[COUNT[a] for a in axes] for axes in AXES]

    def ring(part, stage):
        n = dims[part][stage]
        inner = dims[part][stage + 1 :]
        return pltpu.VMEM((2 * (n - 1), inner[0] // 2, *inner[1:], *tile), F32)

    dma = pltpu.SemaphoreType.DMA
    return pl.pallas_call(
        reduce_kernel,
        out_shape=(
            jax.ShapeDtypeStruct((16, width), BF16),
            jax.ShapeDtypeStruct((28, ZERO * LANES), F32),
            jax.ShapeDtypeStruct((24, 2 * ONE * LANES), F32),
            jax.ShapeDtypeStruct((20, 2 * TWO * LANES), F32),
        ),
        in_specs=[hbm, hbm, vmem],
        out_specs=(vmem,) * 4,
        scratch_shapes=[
            pltpu.VMEM((BLOCKS, LANES, 2 * PADDED), BF16),
            pltpu.VMEM((BLOCKS, 2 * PADDED, LANES), BF16),
            *[pltpu.VMEM((*dims[p], *tile), F32) for p in range(3)],
            *[ring(p, 0) for p in range(3)],
            *[pltpu.VMEM((*dims[p][1:], *tile), F32) for p in range(3)],
            *[ring(p, 1) for p in range(3)],
            *[pltpu.VMEM((dims[p][2], *tile), F32) for p in range(3)],
            *[pltpu.VMEM((dims[p][2] - 1, *tile), F32) for p in range(3)],
            pltpu.VMEM((8, 3 * NK, 8, LANES), F32),
            pltpu.VMEM((NZ, 120, 2 * LANES), F32),
            pltpu.VMEM((2, 8, width), F32),
            dma((5,)), dma((5,)), dma((5,)),
            dma((3, 14)), dma((3, 14)), dma((3, 14)), dma((3, 14)), dma((3, 7)), dma((3, 7)),
            dma((7,)), dma((7,)), dma((2,)), dma((2,)),
        ],
        compiler_params=pltpu.CompilerParams(
            vmem_limit_bytes=VMEM_LIMIT, collective_id=0, has_side_effects=True
        ),
        name="weight_sums",
    )(xt, d, node)


def shards(node_feats, node_cotan, source, target, angle, w_zero, w_one, w_two):
    graphs = lax.axis_size("graph")
    atoms = node_feats.shape[1]
    reach = atoms // 2
    position = lax.axis_index("graph")
    feats, cotan = node_feats[0], node_cotan[0]
    own_low = jnp.concatenate([feats[:reach], cotan[:reach]], 0)
    own_high = jnp.concatenate([feats[reach:], cotan[reach:]], 0)
    from_before = lax.ppermute(own_high, "graph", [(i, (i + 1) % graphs) for i in range(graphs)])
    from_after = lax.ppermute(own_low, "graph", [((i + 1) % graphs, i) for i in range(graphs)])
    table = jnp.concatenate([own_low, own_high, from_before, from_after], 0)

    def table_row(atom):
        local = atom - (position * atoms - reach)
        block = local // reach
        start = jnp.where(block == 0, 32, jnp.where(block == 1, 0, jnp.where(block == 2, 16, 48)))
        return (start + local % reach).astype(F32)

    phases = angle[0]
    zero = jnp.zeros_like(phases)
    rows = jnp.stack(
        [
            jnp.cos(phases), jnp.sin(phases), jnp.cos(2.0 * phases), jnp.sin(2.0 * phases),
            table_row(source[0]), table_row(target[0]) + reach, zero, zero,
        ],
        0,
    )
    xt, d, node = edge_call(rows, table, w_zero, w_one, w_two)
    nodes, zero_g, one_g, two_g = reduce_call(xt, d, node)
    return nodes[None], zero_g, one_g, two_g


def solution(mesh):
    placed = (
        P("dp", "graph", None),
        P("dp", "graph", None),
        P("dp", "graph"),
        P("dp", "graph"),
        P("dp", "graph"),
        P(),
        P(),
        P(),
    )
    return jax.shard_map(
        shards,
        mesh=mesh,
        in_specs=placed,
        out_specs=(P("dp", "graph", None), P("graph", None), P("graph", None), P("graph", None)),
        check_vma=False,
    )
```

```python
import jax
import jax.numpy as jnp
from jax import lax
from jax.experimental import pallas as pl
from jax.experimental.pallas import tpu as pltpu
from jax.sharding import PartitionSpec as P

MESH = pl.DeviceIdType.MESH
F32 = jnp.float32
BF16 = jnp.bfloat16
HEADS = 8
LANES = 128
EDGES = 320
PADDED = 384
BLOCKS = 29
ZERO, ONE, TWO = 7, 6, 5
AT_Z, AT_P1, AT_N1, AT_P2, AT_N2 = 0, 7, 13, 19, 24
VMEM_LIMIT = 62 * 1024 * 1024


def dot(a, b):
    return jnp.dot(a, b, preferred_element_type=F32)


def dot_t(a, b):
    return lax.dot_general(a, b, (((1,), (1,)), ((), ())), preferred_element_type=F32)


def dot_first(a, b):
    return lax.dot_general(a, b, (((0,), (0,)), ((), ())), preferred_element_type=F32)


def split2(v):
    high = v.astype(BF16)
    return high, (v - high.astype(F32)).astype(BF16)


def split3(v):
    high = v.astype(BF16)
    rest = v - high.astype(F32)
    middle = rest.astype(BF16)
    return high, middle, (rest - middle.astype(F32)).astype(BF16)


def chunks(count):
    out, at = [], 0
    while at < count:
        width = min(2, count - at)
        out.append((at, width))
        at += width
    return out


def cols(block, width=1):
    return pl.ds(block * LANES, width * LANES)


def wide(v, width):
    return v if width == 1 else jnp.concatenate([v] * width, axis=1)


def folded(v, width):
    return v if width == 1 else v[:, :LANES] + v[:, LANES:]


SHARES = (
    ((0, 7, 29), (1, 7, 21), (1, 24, 26)),
    ((0, 0, 7), (0, 19, 29), (1, 0, 7), (1, 21, 24), (1, 26, 29)),
)
ONE_ORDER = tuple(b for j in range(3) for b in (2 * j, 2 * j + 1, 6 + 2 * j, 7 + 2 * j))
TILES = (
    tuple((1, i, b) for b in ONE_ORDER for i in range(3)) + tuple((2, i, b) for b in (0, 1, 5, 6) for i in range(3)),
    tuple((0, i, b) for b in range(7) for i in range(4)) + tuple((2, i, b) for b in (2, 3, 4, 7, 8, 9) for i in range(3)),
)
PLACE = tuple({tile: at for at, tile in enumerate(order)} for order in TILES)
NX, NY, NZ = 4, 4, 8
AXES = (("z", "x", "y"), ("x", "y", "z"), ("y", "z", "x"))
TILES_OF = (3, 5, 4)
FIRST_OF = (0, 3, 8)
COUNT = {"x": NX, "y": NY, "z": NZ}


def spot(at):
    part = 0 if at < 4 * FIRST_OF[1] else 1 if at < 4 * FIRST_OF[2] else 2
    inside = at - 4 * FIRST_OF[part]
    return part, inside // TILES_OF[part], inside % TILES_OF[part]


def chains_of(n):
    return ((1, 0, n // 2), (-1, 1, n // 2), (1, 1, n // 2 - 1), (-1, 0, n // 2 - 1))


def edge_kernel(
    feats_ref, cotan_ref, source_ref, target_ref, angle_ref, w0_hbm, w1_hbm, w2_hbm,
    nodes_out, tiles_out,
    w0_ref, w1_ref, w2_ref, tab_ref, x_s, du_s, trig_s, oh_s, node_ref,
    xt_s, d_s, part0, part1, part2, r10, r11, r12, s20, s21, s22, r20, r21, r22, s30, s31, s32, r30, r31, r32,
    gathered, result, node_in,
    load_sem, share_send, share_recv, send1, recv1, send2, recv2, send3, recv3, all_send, all_recv, node_send, node_recv,
    halo_send, halo_recv,
):
    dp = lax.axis_index("dp")
    graph = lax.axis_index("graph")
    core, x = dp % 2, dp // 2
    y, z = graph % NY, graph // NY
    place = {"x": x, "y": y, "z": z}

    def moved(axis, offset):
        n = COUNT[axis]
        to = (place[axis] + offset + n) % n
        if axis == "x":
            return {"dp": to * 2 + core, "graph": graph}
        if axis == "y":
            return {"dp": dp, "graph": z * NY + to}
        return {"dp": dp, "graph": to * NY + y}

    sibling = {"dp": x * 2 + (1 - core), "graph": graph}
    graphs = NY * NZ
    before = {"dp": dp, "graph": (graph + graphs - 1) % graphs}
    after = {"dp": dp, "graph": (graph + 1) % graphs}
    peers = [{"dp": (dp + o) % 8, "graph": graph} for o in range(1, 8)]
    peers += [moved("y", o) for o in range(1, NY)] + [moved("z", o) for o in range(1, NZ)] + [before, after]

    loads = [
        pltpu.make_async_copy(src, dst, load_sem.at[k])
        for k, (src, dst) in enumerate(((w0_hbm, w0_ref), (w1_hbm, w1_ref), (w2_hbm, w2_ref)))
    ]
    for load in loads:
        load.start()
    feats, cotan = feats_ref[...].astype(F32), cotan_ref[...].astype(F32)
    tab_ref[pl.ds(0, 16)] = jnp.concatenate([feats[:8], cotan[:8]], 0).astype(BF16)
    tab_ref[pl.ds(16, 16)] = jnp.concatenate([feats[8:], cotan[8:]], 0).astype(BF16)
    barrier = pltpu.get_barrier_semaphore()
    for peer in peers:
        pl.semaphore_signal(barrier, inc=1, device_id=peer, device_id_type=MESH)
    pl.semaphore_wait(barrier, len(peers))

    def remote(src, dst, send, recv, device):
        return pltpu.make_async_remote_copy(
            src_ref=src, dst_ref=dst, send_sem=send, recv_sem=recv, device_id=device, device_id_type=MESH
        )

    node_up = remote(node_ref.at[pl.ds(0, 8)], node_in.at[1], node_send.at[0], node_recv.at[0], before)
    node_down = remote(node_ref.at[pl.ds(24, 8)], node_in.at[0], node_send.at[1], node_recv.at[1], after)

    def own_half(kind, lo, hi, half):
        if kind == 0:
            return xt_s.at[pl.ds(lo, hi - lo), :, pl.ds(half * PADDED, PADDED)]
        return d_s.at[pl.ds(lo, hi - lo), pl.ds(half * PADDED, PADDED), :]

    def share_copy(k, span):
        return remote(own_half(*span, 0), own_half(*span, 1), share_send.at[k], share_recv.at[k], sibling)

    stage1 = (part0, part1, part2)
    rings1 = (r10, r11, r12)
    stage2 = (s20, s21, s22)
    rings2 = (r20, r21, r22)
    stage3 = (s30, s31, s32)
    slots3 = (r30, r31, r32)

    def slot_of(n, chain, step):
        return sum(c[2] for c in chains_of(n)[:chain]) + step

    def ring_copy(part, stage, chain, step):
        axis = AXES[part][stage]
        n = COUNT[axis]
        way, half, steps = chains_of(n)[chain]
        source, ring = ((stage1, rings1), (stage2, rings2))[stage]
        sends, recvs = ((send1, recv1), (send2, recv2))[stage]
        deep = source[part].shape[1] // 2
        slot = slot_of(n, chain, step)
        if step == 0:
            block = (place[axis] + way * steps + n) % n
            src = source[part].at[block, pl.ds(half * deep, deep)]
        else:
            src = ring[part].at[slot - 1]
        return remote(src, ring[part].at[slot], sends.at[part, slot], recvs.at[part, slot], moved(axis, way))

    def begin(part, stage):
        for chain in range(4):
            ring_copy(part, stage, chain, 0).start()

    def advance(part, stage, step):
        axis = AXES[part][stage]
        n = COUNT[axis]
        source, ring = ((stage1, rings1), (stage2, rings2))[stage]
        deep = source[part].shape[1] // 2
        for chain, (way, half, steps) in enumerate(chains_of(n)):
            if step < steps:
                slot = slot_of(n, chain, step)
                ring_copy(part, stage, chain, step - 1).wait_recv()
                block = (place[axis] + way * (steps - step) + n) % n
                ring[part][slot - 1] = ring[part][slot - 1] + source[part][block, pl.ds(half * deep, deep)]
                ring_copy(part, stage, chain, step).start()

    def finish(part, stage, out):
        axis = AXES[part][stage]
        n = COUNT[axis]
        source, ring = ((stage1, rings1), (stage2, rings2))[stage]
        deep = source[part].shape[1] // 2
        for half in range(2):
            arrived = []
            for chain, (way, h, steps) in enumerate(chains_of(n)):
                if h == half:
                    ring_copy(part, stage, chain, steps - 1).wait_recv()
                    arrived.append(ring[part][slot_of(n, chain, steps - 1)])
            out[pl.ds(half * deep, deep)] = source[part][place[axis], pl.ds(half * deep, deep)] + arrived[0] + arrived[1]

    def sent(part, stage):
        for chain, (way, half, steps) in enumerate(chains_of(COUNT[AXES[part][stage]])):
            for step in range(steps):
                ring_copy(part, stage, chain, step).wait_send()

    def last_copy(part, offset):
        axis = AXES[part][2]
        n = COUNT[axis]
        return remote(
            stage3[part].at[(place[axis] + offset) % n], slots3[part].at[offset - 1],
            send3.at[part, offset - 1], recv3.at[part, offset - 1], moved(axis, offset),
        )

    def last_begin(part):
        for offset in range(1, COUNT[AXES[part][2]]):
            last_copy(part, offset).start()

    def all_copy(part, offset):
        mine = gathered.at[dp, pl.ds(FIRST_OF[part], TILES_OF[part])]
        return remote(
            mine, mine, all_send.at[part, offset - 1], all_recv.at[part, offset - 1],
            {"dp": (dp + offset) % 8, "graph": graph},
        )

    def last_end(part):
        axis = AXES[part][2]
        whole = stage3[part][place[axis]]
        for offset in range(1, COUNT[axis]):
            last_copy(part, offset).wait_recv()
            whole = whole + slots3[part][offset - 1]
        gathered[dp, pl.ds(FIRST_OF[part], TILES_OF[part])] = whole
        for offset in range(1, 8):
            all_copy(part, offset).start()

    def put(which, tile, row_y, v):
        at = PLACE[which][tile]
        part, px, pk = spot(at)
        if part == 0:
            part0[:, px, row_y, pk] = v
        elif part == 1:
            part1[px, row_y, :, pk] = v
        else:
            part2[row_y, :, px, pk] = v

    def pair(block, width):
        return jnp.concatenate([d_s[block + k] for k in range(width)], axis=1)

    def factor(block, count):
        return xt_s[pl.ds(block, count)].reshape(count * LANES, 2 * PADDED)

    def put_aligned(v, first_blocks):
        shaped = v.reshape(NZ, NY * 3, 8, v.shape[1])
        for w, b in enumerate(first_blocks):
            for row_y in range(NY):
                for i in range(3):
                    put(0, (1, i, b), row_y, shaped[:, row_y * 3 + i, :, w * LANES : (w + 1) * LANES])

    def put_shifted(which, matrix, tiles, shard, v, first_blocks):
        result[:, pl.ds(0, NY * shard), pl.ds(0, v.shape[1])] = v.reshape(NZ, NY * shard, v.shape[1])
        for w, b in enumerate(first_blocks):
            for row_y in range(NY):
                for i in range(tiles):
                    put(which, (matrix, i, b), row_y, result[:, pl.ds(row_y * shard + i * 8, 8), cols(w)])

    def two_blocks(which, at, width):
        dp_, dn_ = pair(AT_P2 + at, width), pair(AT_N2 + at, width)
        rp, rn = factor(AT_P2, TWO), factor(AT_N2, TWO)
        put_shifted(which, 2, 3, 20, dot(rp, dp_) + dot(rn, dn_), range(at, at + width))
        put_shifted(which, 2, 3, 20, dot(rp, dn_) - dot(rn, dp_), range(TWO + at, TWO + at + width))


    halo_down = remote(tab_ref.at[pl.ds(16, 16)], tab_ref.at[pl.ds(32, 16)], halo_send.at[0], halo_recv.at[0], after)
    halo_up = remote(tab_ref.at[pl.ds(0, 16)], tab_ref.at[pl.ds(48, 16)], halo_send.at[1], halo_recv.at[1], before)
    halo_down.start()
    halo_up.start()

    first_atom = graph * 16 - 8

    def table_row(atoms, shift):
        local = atoms - first_atom
        block = local >> 3
        base = jnp.where(block == 0, 32, jnp.where(block == 1, 0, jnp.where(block == 2, 16, 48)))
        return (base + (local & 7) + shift).astype(F32)

    row = lax.broadcasted_iota(jnp.int32, (8, EDGES), 0)
    phases = jnp.broadcast_to(angle_ref[...], (8, EDGES))
    phases = jnp.where(row < 2, phases, 2.0 * phases)
    ends = jnp.where(row == 4, table_row(source_ref[...], 0), table_row(target_ref[...], 8))
    rows = jnp.where(row >= 4, ends, jnp.where((row & 1) == 0, jnp.cos(phases), jnp.sin(phases)))
    parts = jnp.concatenate(list(split3(rows)), axis=0)
    pick_row = lax.broadcasted_iota(jnp.int32, (24, 6 * LANES), 0)
    pick_col = lax.broadcasted_iota(jnp.int32, (24, 6 * LANES), 1)
    chosen = jnp.where(pick_row % 8 == pick_col // LANES, 1.0, 0.0).astype(BF16)
    spread = dot_first(parts, chosen)
    for k in range(4):
        trig_s[k] = spread[:, k * LANES : (k + 1) * LANES]
    lane = lax.broadcasted_iota(jnp.int32, (EDGES, LANES), 1).astype(F32)
    for k in range(2):
        oh_s[k] = jnp.where(spread[:, (4 + k) * LANES : (5 + k) * LANES] == lane, 1.0, 0.0).astype(BF16)
    depth = tab_ref.shape[0]
    oh_src = oh_s[0, :, :depth]
    oh_dst = oh_s[1, :, :depth]

    xt_s[:, :, EDGES:PADDED] = jnp.zeros((BLOCKS, LANES, PADDED - EDGES), BF16)
    d_s[:, EDGES:PADDED, :] = jnp.zeros((BLOCKS, PADDED - EDGES, LANES), BF16)
    result[...] = jnp.zeros_like(result)
    halo_down.wait_recv()
    halo_up.wait_recv()

    def keep_x(block, width, v):
        x_s[:, cols(block, width)] = v
        for w in range(width):
            xt_s[block + w, :, :EDGES] = v[:, w * LANES : (w + 1) * LANES].T

    def rotated(onehot, c, s, plus, minus, width):
        a = dot(onehot, tab_ref[:, cols(plus, width)])
        b = dot(onehot, tab_ref[:, cols(minus, width)])
        return c * a - s * b, s * a + c * b

    for at, width in chunks(ZERO):
        keep_x(at, width, dot(oh_src, tab_ref[:, cols(at, width)]).astype(BF16))
    for m, (count, plus, minus) in enumerate(((ONE, AT_P1, AT_N1), (TWO, AT_P2, AT_N2))):
        for at, width in chunks(count):
            c, s = wide(trig_s[2 * m], width), wide(trig_s[2 * m + 1], width)
            p, n = rotated(oh_src, c, s, plus + at, minus + at, width)
            keep_x(plus + at, width, p.astype(BF16))
            keep_x(minus + at, width, n.astype(BF16))


    def share(kind):
        @pl.when(core == 0)
        def _():
            for k, span in enumerate(SHARES[1]):
                if span[0] == kind:
                    share_copy(k, span).start()

        @pl.when(core == 1)
        def _():
            for k, span in enumerate(SHARES[0]):
                if span[0] == kind:
                    share_copy(k, span).start()

    share(0)
    for load in loads:
        load.wait()
    total = jnp.zeros((EDGES, LANES), F32)
    first = None
    for at, width in chunks(ZERO):
        out = dot(x_s[:, cols(0, ZERO)], w0_ref[:, cols(at, width)])
        if at == 0:
            first = out[:, :LANES]
        up = dot(oh_dst, tab_ref[:, cols(at, width)])
        du_s[:, cols(at, width)] = up
        total = total + folded(up * out, width)
    for m, (count, plus, minus, w_ref) in enumerate(((ONE, AT_P1, AT_N1, w1_ref), (TWO, AT_P2, AT_N2, w2_ref))):
        for at, width in chunks(count):
            c, s = wide(trig_s[2 * m], width), wide(trig_s[2 * m + 1], width)
            up_p, up_n = rotated(oh_dst, c, s, plus + at, minus + at, width)
            du_s[:, cols(plus + at, width)] = up_p
            du_s[:, cols(minus + at, width)] = up_n
            xp, xn = x_s[:, cols(plus, count)], x_s[:, cols(minus, count)]
            left, right = w_ref[:, cols(at, width)], w_ref[:, cols(count + at, width)]
            out_p = dot(xp, left) - dot(xn, right)
            out_n = dot(xp, right) + dot(xn, left)
            total = total + folded(up_p * out_p + up_n * out_n, width)

    size = LANES // HEADS
    head_r = lax.broadcasted_iota(jnp.int32, (LANES, LANES), 0) // size
    head_c = lax.broadcasted_iota(jnp.int32, (LANES, LANES), 1) // size
    same = jnp.where(head_r == head_c, 1.0, 0.0).astype(BF16)

    def head_sum(v):
        high, middle, low = split3(v)
        return dot(low, same) + dot(middle, same) + dot(high, same)

    scale = 1.0 / (float(size) ** 0.5)
    gate = jax.nn.sigmoid(head_sum(first) * scale)
    dlogit = head_sum(total) * gate * (1.0 - gate) * scale
    for block in range(BLOCKS):
        v = du_s[:, cols(block)] * gate
        if block == 0:
            v = v + dlogit
        d_s[block, :EDGES, :] = v.astype(BF16)

    share(1)


    @pl.when(core == 0)
    def _():
        for k, span in enumerate(SHARES[0]):
            share_copy(k, span).wait_recv()
        for j in range(3):
            dp_, dn_ = pair(AT_P1 + 2 * j, 2), pair(AT_N1 + 2 * j, 2)
            rp, rn = factor(AT_P1, ONE), factor(AT_N1, ONE)
            put_aligned(dot(rp, dp_) + dot(rn, dn_), (2 * j, 2 * j + 1))
            put_aligned(dot(rp, dn_) - dot(rn, dp_), (6 + 2 * j, 7 + 2 * j))
            if j == 0:
                begin(0, 0)
        begin(1, 0)
        two_blocks(0, 0, 2)
        begin(2, 0)
        for k, span in enumerate(SHARES[1]):
            share_copy(k, span).wait_send()

    @pl.when(core == 1)
    def _():
        for k, span in enumerate(SHARES[1]):
            share_copy(k, span).wait_recv()
        blank = jnp.zeros((NZ, 8, LANES), F32)
        for row_y in range(NY):
            for k in (2, 3):
                part2[row_y, :, 3, k] = blank
        for at, width in chunks(ZERO):
            put_shifted(1, 0, 4, 28, dot(factor(AT_Z, ZERO), pair(AT_Z + at, width)), range(at, at + width))
            if at == 2:
                begin(0, 0)
        two_blocks(1, 2, 2)
        begin(1, 0)
        two_blocks(1, 4, 1)
        begin(2, 0)
        for k, span in enumerate(SHARES[0]):
            share_copy(k, span).wait_send()

    atoms = node_ref.shape[0]
    atom = lax.broadcasted_iota(jnp.int32, (atoms, EDGES), 0)
    table_row = jnp.where(atom < 8, atom + 32, jnp.where(atom < 16, atom - 8, jnp.where(atom < 24, atom, atom + 24)))
    oh_rows = jnp.where(table_row.astype(F32) == rows[4:5, :], 1.0, 0.0).astype(BF16)

    def scatter(block, width, v):
        high, low = split2(v)
        node_ref[:, cols(block, width)] = dot(oh_rows, high) + dot(oh_rows, low)

    def dconv(block, count):
        return jnp.concatenate([d_s[block + k, :EDGES, :] for k in range(count)], axis=1)

    dz = dconv(AT_Z, ZERO)
    for at, width in chunks(ZERO):
        scatter(at, width, dot_t(dz, w0_ref[cols(at, width), :]))
    for m, (count, plus, minus, w_ref) in enumerate(((ONE, AT_P1, AT_N1, w1_ref), (TWO, AT_P2, AT_N2, w2_ref))):
        gp, gn = dconv(plus, count), dconv(minus, count)
        for at, width in chunks(count):
            c, s = wide(trig_s[2 * m], width), wide(trig_s[2 * m + 1], width)
            left, right = w_ref[cols(at, width), cols(0, count)], w_ref[cols(at, width), cols(count, count)]
            back_p = dot_t(gp, left) + dot_t(gn, right)
            back_n = dot_t(gn, left) - dot_t(gp, right)
            scatter(plus + at, width, c * back_p + s * back_n)
            scatter(minus + at, width, c * back_n - s * back_p)


    node_up.start()
    node_down.start()

    for part in (1, 2):
        advance(part, 0, 1)
    advance(0, 0, 1)
    advance(0, 0, 2)
    node_up.wait()
    node_down.wait()
    nodes_out[pl.ds(0, 8)] = (node_ref[pl.ds(8, 8)] + node_in[0]).astype(BF16)
    nodes_out[pl.ds(8, 8)] = (node_ref[pl.ds(16, 8)] + node_in[1]).astype(BF16)
    advance(0, 0, 3)
    finish(1, 0, s21)
    begin(1, 1)
    finish(2, 0, s22)
    begin(2, 1)
    finish(0, 0, s20)
    begin(0, 1)
    advance(1, 1, 1)
    advance(2, 1, 1)
    advance(0, 1, 1)
    finish(1, 1, s31)
    last_begin(1)
    advance(2, 1, 2)
    finish(0, 1, s30)
    last_begin(0)
    advance(2, 1, 3)
    last_end(0)
    last_end(1)
    finish(2, 1, s32)
    last_begin(2)
    last_end(2)
    for part in range(3):
        for stage in range(2):
            sent(part, stage)
        for offset in range(1, COUNT[AXES[part][2]]):
            last_copy(part, offset).wait_send()
    for part in range(3):
        for offset in range(1, 8):
            all_copy(part, offset).wait_recv()
    tiles_out[...] = gathered[...] * 0.125
    for part in range(3):
        for offset in range(1, 8):
            all_copy(part, offset).wait_send()
    halo_down.wait_send()
    halo_up.wait_send()


def place_kernel(tiles_ref, nodes_ref, nodes_out, zero_out, one_out, two_out):
    nodes_out[...] = nodes_ref[...]
    outs = (zero_out, one_out, two_out)
    for which in range(2):
        for at, (matrix, i, b) in enumerate(TILES[which]):
            part, px, pk = spot(at)
            out = outs[matrix]
            rows = min(8, out.shape[0] - 8 * i)
            out[pl.ds(8 * i, rows), cols(b)] = tiles_ref[px * 2 + which, FIRST_OF[part] + pk, pl.ds(0, rows)]


def shards(node_feats, node_cotan, source, target, angle, w_zero, w_one, w_two):
    width = node_feats.shape[2]
    vmem = pl.BlockSpec(memory_space=pltpu.VMEM)
    hbm = pl.BlockSpec(memory_space=pl.ANY)
    dims = [[COUNT[a] for a in axes] for axes in AXES]
    tile = [(k, 8, LANES) for k in TILES_OF]

    def ring(part, stage):
        n = dims[part][stage]
        inner = dims[part][stage + 1 :]
        return pltpu.VMEM((2 * (n - 1), inner[0] // 2, *inner[1:], *tile[part]), F32)

    dma = pltpu.SemaphoreType.DMA
    nodes, tiles = pl.pallas_call(
        edge_kernel,
        out_shape=(
            jax.ShapeDtypeStruct((16, width), BF16),
            jax.ShapeDtypeStruct((8, 12, 8, LANES), F32),
        ),
        in_specs=[vmem] * 5 + [hbm] * 3,
        out_specs=(vmem,) * 2,
        scratch_shapes=[
            pltpu.VMEM(w_zero.shape, BF16),
            pltpu.VMEM(w_one.shape, BF16),
            pltpu.VMEM(w_two.shape, BF16),
            pltpu.VMEM((64, width), BF16),
            pltpu.VMEM((EDGES, width), BF16),
            pltpu.VMEM((EDGES, width), F32),
            pltpu.VMEM((4, EDGES, LANES), F32),
            pltpu.VMEM((2, EDGES, LANES), BF16),
            pltpu.VMEM((32, width), F32),
            pltpu.VMEM((BLOCKS, LANES, 2 * PADDED), BF16),
            pltpu.VMEM((BLOCKS, 2 * PADDED, LANES), BF16),
            *[pltpu.VMEM((*dims[p], *tile[p]), F32) for p in range(3)],
            *[ring(p, 0) for p in range(3)],
            *[pltpu.VMEM((*dims[p][1:], *tile[p]), F32) for p in range(3)],
            *[ring(p, 1) for p in range(3)],
            *[pltpu.VMEM((dims[p][2], *tile[p]), F32) for p in range(3)],
            *[pltpu.VMEM((dims[p][2] - 1, *tile[p]), F32) for p in range(3)],
            pltpu.VMEM((8, 12, 8, LANES), F32),
            pltpu.VMEM((NZ, 120, 2 * LANES), F32),
            pltpu.VMEM((2, 8, width), F32),
            dma((3,)), dma((5,)), dma((5,)),
            dma((3, 14)), dma((3, 14)), dma((3, 14)), dma((3, 14)), dma((3, 7)), dma((3, 7)),
            dma((3, 7)), dma((3, 7)), dma((2,)), dma((2,)), dma((2,)), dma((2,)),
        ],
        compiler_params=pltpu.CompilerParams(
            vmem_limit_bytes=VMEM_LIMIT, collective_id=0, has_side_effects=True
        ),
        name="edge_gradients",
    )(node_feats[0], node_cotan[0], source, target, angle, w_zero, w_one, w_two)
    nodes, zero_g, one_g, two_g = pl.pallas_call(
        place_kernel,
        out_shape=(
            jax.ShapeDtypeStruct((16, width), BF16),
            jax.ShapeDtypeStruct((28, ZERO * LANES), F32),
            jax.ShapeDtypeStruct((24, 2 * ONE * LANES), F32),
            jax.ShapeDtypeStruct((20, 2 * TWO * LANES), F32),
        ),
        in_specs=[vmem] * 2,
        out_specs=(vmem,) * 4,
        name="place_tiles",
    )(tiles, nodes)
    return nodes[None], zero_g, one_g, two_g


def solution(mesh):
    placed = (
        P("dp", "graph", None),
        P("dp", "graph", None),
        P("dp", "graph"),
        P("dp", "graph"),
        P("dp", "graph"),
        P(),
        P(),
        P(),
    )
    return jax.shard_map(
        shards,
        mesh=mesh,
        in_specs=placed,
        out_specs=(P("dp", "graph", None), P("graph", None), P("graph", None), P("graph", None)),
        check_vma=False,
    )
```

```python
import jax
import jax.numpy as jnp
from jax import lax
from jax.experimental import pallas as pl
from jax.experimental.pallas import tpu as pltpu
from jax.sharding import PartitionSpec as P

MESH = pl.DeviceIdType.MESH
F32 = jnp.float32
BF16 = jnp.bfloat16
HEADS = 8
LANES = 128
EDGES = 320
PADDED = 384
BLOCKS = 29
ZERO, ONE, TWO = 7, 6, 5
AT_Z, AT_P1, AT_N1, AT_P2, AT_N2 = 0, 7, 13, 19, 24
VMEM_LIMIT = 62 * 1024 * 1024


def dot(a, b):
    return jnp.dot(a, b, preferred_element_type=F32)


def dot_t(a, b):
    return lax.dot_general(a, b, (((1,), (1,)), ((), ())), preferred_element_type=F32)


def dot_first(a, b):
    return lax.dot_general(a, b, (((0,), (0,)), ((), ())), preferred_element_type=F32)


def split2(v):
    high = v.astype(BF16)
    return high, (v - high.astype(F32)).astype(BF16)


def split3(v):
    high = v.astype(BF16)
    rest = v - high.astype(F32)
    middle = rest.astype(BF16)
    return high, middle, (rest - middle.astype(F32)).astype(BF16)


def chunks(count):
    out, at = [], 0
    while at < count:
        width = min(2, count - at)
        out.append((at, width))
        at += width
    return out


def cols(block, width=1):
    return pl.ds(block * LANES, width * LANES)


def wide(v, width):
    return v if width == 1 else jnp.concatenate([v] * width, axis=1)


def folded(v, width):
    return v if width == 1 else v[:, :LANES] + v[:, LANES:]


SHARES = (
    ((0, 7, 29), (1, 7, 21), (1, 24, 26)),
    ((0, 0, 7), (0, 19, 29), (1, 0, 7), (1, 21, 24), (1, 26, 29)),
)
ONE_ORDER = tuple(b for j in range(3) for b in (2 * j, 2 * j + 1, 6 + 2 * j, 7 + 2 * j))
TILES = (
    tuple((1, i, b) for b in ONE_ORDER for i in range(3)) + tuple((2, i, b) for b in (0, 1, 5, 6) for i in range(3)),
    tuple((0, i, b) for b in range(7) for i in range(4)) + tuple((2, i, b) for b in (2, 3, 4, 7, 8, 9) for i in range(3)),
)
PLACE = tuple({tile: at for at, tile in enumerate(order)} for order in TILES)
NX, NY, NZ = 4, 4, 8
AXES = (("z", "x", "y"), ("x", "y", "z"), ("y", "x", "z"))
TILES_OF = (3, 4, 5)
FIRST_OF = (0, TILES_OF[0], TILES_OF[0] + TILES_OF[1])
COUNT = {"x": NX, "y": NY, "z": NZ}


def spot(at):
    part = 0 if at < 4 * FIRST_OF[1] else 1 if at < 4 * FIRST_OF[2] else 2
    inside = at - 4 * FIRST_OF[part]
    return part, inside // TILES_OF[part], inside % TILES_OF[part]


def chains_of(n):
    return ((1, 0, n // 2), (-1, 1, n // 2), (1, 1, n // 2 - 1), (-1, 0, n // 2 - 1))


def edge_kernel(
    feats_ref, cotan_ref, source_ref, target_ref, angle_ref, w0_hbm, w1_hbm, w2_hbm,
    nodes_out, tiles_out,
    w0_ref, w1_ref, w2_ref, tab_ref, x_s, du_s, trig_s, oh_s, node_ref,
    xt_s, d_s, part0, part1, part2, r10, r11, r12, s20, s21, s22, r20, r21, r22, s30, s31, s32, r30, r31, r32,
    o0, o1, o2, i0, i1, i2, gathered, result, node_in,
    load_sem, share_send, share_recv, send1, recv1, send2, recv2, send3, recv3, all_send, all_recv, node_send, node_recv,
    halo_send, halo_recv,
):
    dp = lax.axis_index("dp")
    graph = lax.axis_index("graph")
    core, x = dp % 2, dp // 2
    y, z = graph % NY, graph // NY
    place = {"x": x, "y": y, "z": z}

    def moved(axis, offset):
        n = COUNT[axis]
        to = (place[axis] + offset + n) % n
        if axis == "x":
            return {"dp": to * 2 + core, "graph": graph}
        if axis == "y":
            return {"dp": dp, "graph": z * NY + to}
        return {"dp": dp, "graph": to * NY + y}

    sibling = {"dp": x * 2 + (1 - core), "graph": graph}
    graphs = NY * NZ
    before = {"dp": dp, "graph": (graph + graphs - 1) % graphs}
    after = {"dp": dp, "graph": (graph + 1) % graphs}
    peers = [{"dp": (dp + o) % 8, "graph": graph} for o in range(1, 8)]
    peers += [moved("y", o) for o in range(1, NY)] + [moved("z", o) for o in range(1, NZ)] + [before, after]

    barrier = pltpu.get_barrier_semaphore()
    for peer in peers:
        pl.semaphore_signal(barrier, inc=1, device_id=peer, device_id_type=MESH)
    loads = [
        pltpu.make_async_copy(src, dst, load_sem.at[k])
        for k, (src, dst) in enumerate(((w0_hbm, w0_ref), (w1_hbm, w1_ref), (w2_hbm, w2_ref)))
    ]
    for load in loads:
        load.start()
    feats, cotan = feats_ref[...].astype(F32), cotan_ref[...].astype(F32)
    tab_ref[pl.ds(0, 16)] = jnp.concatenate([feats[:8], cotan[:8]], 0).astype(BF16)
    tab_ref[pl.ds(16, 16)] = jnp.concatenate([feats[8:], cotan[8:]], 0).astype(BF16)
    def remote(src, dst, send, recv, device):
        return pltpu.make_async_remote_copy(
            src_ref=src, dst_ref=dst, send_sem=send, recv_sem=recv, device_id=device, device_id_type=MESH
        )

    node_up = remote(node_ref.at[pl.ds(0, 8)], node_in.at[1], node_send.at[0], node_recv.at[0], before)
    node_down = remote(node_ref.at[pl.ds(24, 8)], node_in.at[0], node_send.at[1], node_recv.at[1], after)

    def own_half(kind, lo, hi, half):
        if kind == 0:
            return xt_s.at[pl.ds(lo, hi - lo), :, pl.ds(half * PADDED, PADDED)]
        return d_s.at[pl.ds(lo, hi - lo), pl.ds(half * PADDED, PADDED), :]

    def share_copy(k, span):
        return remote(own_half(*span, 0), own_half(*span, 1), share_send.at[k], share_recv.at[k], sibling)

    stage1 = (part0, part1, part2)
    rings1 = (r10, r11, r12)
    stage2 = (s20, s21, s22)
    rings2 = (r20, r21, r22)
    stage3 = (s30, s31, s32)
    slots3 = (r30, r31, r32)

    outs16, ins16 = (o0, o1, o2), (i0, i1, i2)

    def slot_of(n, chain, step):
        return sum(c[2] for c in chains_of(n)[:chain]) + step

    def ring_copy(part, stage, chain, step):
        axis = AXES[part][stage]
        n = COUNT[axis]
        way, half, steps = chains_of(n)[chain]
        source, ring = ((stage1, rings1), (stage2, rings2))[stage]
        sends, recvs = ((send1, recv1), (send2, recv2))[stage]
        deep = source[part].shape[1] // 2
        slot = slot_of(n, chain, step)
        if step == 0 and stage == 0:
            return remote(
                outs16[part].at[chain], ins16[part].at[chain],
                sends.at[part, slot], recvs.at[part, slot], moved(axis, way),
            )
        if step == 0:
            block = (place[axis] + way * steps + n) % n
            src = source[part].at[block, pl.ds(half * deep, deep)]
        else:
            src = ring[part].at[slot - 1]
        return remote(src, ring[part].at[slot], sends.at[part, slot], recvs.at[part, slot], moved(axis, way))

    def begin(part, stage):
        axis = AXES[part][stage]
        n = COUNT[axis]
        for chain, (way, half, steps) in enumerate(chains_of(n)):
            if stage == 0:
                deep = stage1[part].shape[1] // 2
                block = (place[axis] + way * steps + n) % n
                v = stage1[part][block, pl.ds(half * deep, deep)]
                outs16[part][chain] = v.reshape(outs16[part].shape[1:]).astype(BF16)
            ring_copy(part, stage, chain, 0).start()

    def arrival(part, stage, chain, step):
        n = COUNT[AXES[part][stage]]
        ring = (rings1, rings2)[stage][part]
        if stage == 0 and step == 0:
            return ins16[part][chain].astype(F32).reshape(ring.shape[1:])
        return ring[slot_of(n, chain, step)]

    def advance(part, stage, step):
        axis = AXES[part][stage]
        n = COUNT[axis]
        source, ring = ((stage1, rings1), (stage2, rings2))[stage]
        deep = source[part].shape[1] // 2
        for chain, (way, half, steps) in enumerate(chains_of(n)):
            if step < steps:
                slot = slot_of(n, chain, step)
                ring_copy(part, stage, chain, step - 1).wait_recv()
                block = (place[axis] + way * (steps - step) + n) % n
                ring[part][slot - 1] = arrival(part, stage, chain, step - 1) + source[part][block, pl.ds(half * deep, deep)]
                ring_copy(part, stage, chain, step).start()

    def finish(part, stage, out):
        axis = AXES[part][stage]
        n = COUNT[axis]
        source, ring = ((stage1, rings1), (stage2, rings2))[stage]
        deep = source[part].shape[1] // 2
        for half in range(2):
            arrived = []
            for chain, (way, h, steps) in enumerate(chains_of(n)):
                if h == half:
                    ring_copy(part, stage, chain, steps - 1).wait_recv()
                    arrived.append(arrival(part, stage, chain, steps - 1))
            out[pl.ds(half * deep, deep)] = source[part][place[axis], pl.ds(half * deep, deep)] + arrived[0] + arrived[1]

    def sent(part, stage):
        for chain, (way, half, steps) in enumerate(chains_of(COUNT[AXES[part][stage]])):
            for step in range(steps):
                ring_copy(part, stage, chain, step).wait_send()

    def last_copy(part, offset):
        axis = AXES[part][2]
        n = COUNT[axis]
        return remote(
            stage3[part].at[(place[axis] + offset) % n], slots3[part].at[offset - 1],
            send3.at[part, offset - 1], recv3.at[part, offset - 1], moved(axis, offset),
        )

    def last_begin(part):
        for offset in range(1, COUNT[AXES[part][2]]):
            last_copy(part, offset).start()

    def all_copy(part, offset):
        mine = gathered.at[dp, pl.ds(FIRST_OF[part], TILES_OF[part])]
        return remote(
            mine, mine, all_send.at[part, offset - 1], all_recv.at[part, offset - 1],
            {"dp": (dp + offset) % 8, "graph": graph},
        )

    def last_end(part):
        axis = AXES[part][2]
        whole = stage3[part][place[axis]]
        for offset in range(1, COUNT[axis]):
            last_copy(part, offset).wait_recv()
            whole = whole + slots3[part][offset - 1]
        gathered[dp, pl.ds(FIRST_OF[part], TILES_OF[part])] = whole
        for offset in range(1, 8):
            all_copy(part, offset).start()

    def ready(had, have):
        for part in range(3):
            if had < 4 * (FIRST_OF[part] + TILES_OF[part]) <= have:
                begin(part, 0)

    def put(which, tile, row_y, v):
        at = PLACE[which][tile]
        part, px, pk = spot(at)
        if part == 0:
            part0[:, px, row_y, pk] = v
        elif part == 1:
            part1[px, row_y, :, pk] = v
        else:
            part2[row_y, px, :, pk] = v

    def pair(block, width):
        return jnp.concatenate([d_s[block + k] for k in range(width)], axis=1)

    def factor(block, count):
        return xt_s[pl.ds(block, count)].reshape(count * LANES, 2 * PADDED)

    def put_aligned(v, first_blocks):
        shaped = v.reshape(NZ, NY * 3, 8, v.shape[1])
        for w, b in enumerate(first_blocks):
            for row_y in range(NY):
                for i in range(3):
                    put(0, (1, i, b), row_y, shaped[:, row_y * 3 + i, :, w * LANES : (w + 1) * LANES])

    def put_shifted(which, matrix, tiles, shard, v, first_blocks):
        result[:, pl.ds(0, NY * shard), pl.ds(0, v.shape[1])] = v.reshape(NZ, NY * shard, v.shape[1])
        for w, b in enumerate(first_blocks):
            for row_y in range(NY):
                for i in range(tiles):
                    put(which, (matrix, i, b), row_y, result[:, pl.ds(row_y * shard + i * 8, 8), cols(w)])

    def two_blocks(which, at, width):
        dp_, dn_ = pair(AT_P2 + at, width), pair(AT_N2 + at, width)
        rp, rn = factor(AT_P2, TWO), factor(AT_N2, TWO)
        put_shifted(which, 2, 3, 20, dot(rp, dp_) + dot(rn, dn_), range(at, at + width))
        put_shifted(which, 2, 3, 20, dot(rp, dn_) - dot(rn, dp_), range(TWO + at, TWO + at + width))


    orders = ((0, AT_P1), (AT_P1, AT_P2), (AT_P2, BLOCKS))

    def halo_copies(k):
        span = pl.ds(orders[k][0] * LANES, (orders[k][1] - orders[k][0]) * LANES)
        return (
            remote(
                tab_ref.at[pl.ds(16, 16), span], tab_ref.at[pl.ds(32, 16), span],
                halo_send.at[k, 0], halo_recv.at[k, 0], after,
            ),
            remote(
                tab_ref.at[pl.ds(0, 16), span], tab_ref.at[pl.ds(48, 16), span],
                halo_send.at[k, 1], halo_recv.at[k, 1], before,
            ),
        )

    first_atom = graph * 16 - 8

    def table_row(atoms, shift):
        local = atoms - first_atom
        block = local >> 3
        base = jnp.where(block == 0, 32, jnp.where(block == 1, 0, jnp.where(block == 2, 16, 48)))
        return (base + (local & 7) + shift).astype(F32)

    row = lax.broadcasted_iota(jnp.int32, (8, EDGES), 0)
    phases = jnp.broadcast_to(angle_ref[...], (8, EDGES))
    phases = jnp.where(row < 2, phases, 2.0 * phases)
    ends = jnp.where(row == 4, table_row(source_ref[...], 0), table_row(target_ref[...], 8))
    rows = jnp.where(row >= 4, ends, jnp.where((row & 1) == 0, jnp.cos(phases), jnp.sin(phases)))
    parts = jnp.concatenate(list(split3(rows)), axis=0)
    pick_row = lax.broadcasted_iota(jnp.int32, (24, 6 * LANES), 0)
    pick_col = lax.broadcasted_iota(jnp.int32, (24, 6 * LANES), 1)
    chosen = jnp.where(pick_row % 8 == pick_col // LANES, 1.0, 0.0).astype(BF16)
    spread = dot_first(parts, chosen)
    for k in range(4):
        trig_s[k] = spread[:, k * LANES : (k + 1) * LANES]
    lane = lax.broadcasted_iota(jnp.int32, (EDGES, LANES), 1).astype(F32)
    for k in range(2):
        oh_s[k] = jnp.where(spread[:, (4 + k) * LANES : (5 + k) * LANES] == lane, 1.0, 0.0).astype(BF16)
    depth = tab_ref.shape[0]
    oh_src = oh_s[0, :, :depth]
    oh_dst = oh_s[1, :, :depth]

    pl.semaphore_wait(barrier, len(peers))

    for k in range(3):
        for copy in halo_copies(k):
            copy.start()
    xt_s[:, :, EDGES:PADDED] = jnp.zeros((BLOCKS, LANES, PADDED - EDGES), BF16)
    d_s[:, EDGES:PADDED, :] = jnp.zeros((BLOCKS, PADDED - EDGES, LANES), BF16)
    result[...] = jnp.zeros_like(result)

    def keep_x(block, width, v):
        x_s[:, cols(block, width)] = v
        for w in range(width):
            xt_s[block + w, :, :EDGES] = v[:, w * LANES : (w + 1) * LANES].T

    def rotated(onehot, c, s, plus, minus, width):
        a = dot(onehot, tab_ref[:, cols(plus, width)])
        b = dot(onehot, tab_ref[:, cols(minus, width)])
        return c * a - s * b, s * a + c * b

    for copy in halo_copies(0):
        copy.wait_recv()
    for at, width in chunks(ZERO):
        keep_x(at, width, dot(oh_src, tab_ref[:, cols(at, width)]).astype(BF16))
    for m, (count, plus, minus) in enumerate(((ONE, AT_P1, AT_N1), (TWO, AT_P2, AT_N2))):
        for copy in halo_copies(1 + m):
            copy.wait_recv()
        for at, width in chunks(count):
            c, s = wide(trig_s[2 * m], width), wide(trig_s[2 * m + 1], width)
            p, n = rotated(oh_src, c, s, plus + at, minus + at, width)
            keep_x(plus + at, width, p.astype(BF16))
            keep_x(minus + at, width, n.astype(BF16))


    def share(kind, lo, hi):
        for other in range(2):
            @pl.when(core == 1 - other)
            def _(other=other):
                for k, span in enumerate(SHARES[other]):
                    if span[0] == kind and lo < span[2] <= hi:
                        share_copy(k, span).start()

    share(0, 0, BLOCKS)
    for load in loads:
        load.wait()
    total = jnp.zeros((EDGES, LANES), F32)
    first = None
    for at, width in chunks(ZERO):
        out = dot(x_s[:, cols(0, ZERO)], w0_ref[:, cols(at, width)])
        if at == 0:
            first = out[:, :LANES]
        up = dot(oh_dst, tab_ref[:, cols(at, width)])
        du_s[:, cols(at, width)] = up
        total = total + folded(up * out, width)
    for m, (count, plus, minus, w_ref) in enumerate(((ONE, AT_P1, AT_N1, w1_ref), (TWO, AT_P2, AT_N2, w2_ref))):
        for at, width in chunks(count):
            c, s = wide(trig_s[2 * m], width), wide(trig_s[2 * m + 1], width)
            up_p, up_n = rotated(oh_dst, c, s, plus + at, minus + at, width)
            du_s[:, cols(plus + at, width)] = up_p
            du_s[:, cols(minus + at, width)] = up_n
            xp, xn = x_s[:, cols(plus, count)], x_s[:, cols(minus, count)]
            left, right = w_ref[:, cols(at, width)], w_ref[:, cols(count + at, width)]
            out_p = dot(xp, left) - dot(xn, right)
            out_n = dot(xp, right) + dot(xn, left)
            total = total + folded(up_p * out_p + up_n * out_n, width)

    size = LANES // HEADS
    head_r = lax.broadcasted_iota(jnp.int32, (LANES, LANES), 0) // size
    head_c = lax.broadcasted_iota(jnp.int32, (LANES, LANES), 1) // size
    same = jnp.where(head_r == head_c, 1.0, 0.0).astype(BF16)

    def head_sum(v):
        high, middle, low = split3(v)
        return dot(low, same) + dot(middle, same) + dot(high, same)

    scale = 1.0 / (float(size) ** 0.5)
    gate = jax.nn.sigmoid(head_sum(first) * scale)
    dlogit = head_sum(total) * gate * (1.0 - gate) * scale
    for block in range(BLOCKS):
        v = du_s[:, cols(block)] * gate
        if block == 0:
            v = v + dlogit
        d_s[block, :EDGES, :] = v.astype(BF16)
        if any(block + 1 == span[2] for spans in SHARES for span in spans if span[0]):
            share(1, block, block + 1)


    atoms = node_ref.shape[0]
    atom = lax.broadcasted_iota(jnp.int32, (atoms, EDGES), 0)
    table_row = jnp.where(atom < 8, atom + 32, jnp.where(atom < 16, atom - 8, jnp.where(atom < 24, atom, atom + 24)))
    oh_rows = jnp.where(table_row.astype(F32) == rows[4:5, :], 1.0, 0.0).astype(BF16)

    def scatter(block, width, v):
        high, low = split2(v)
        node_ref[:, cols(block, width)] = dot(oh_rows, high) + dot(oh_rows, low)

    def dconv(block, count):
        return jnp.concatenate([d_s[block + k, :EDGES, :] for k in range(count)], axis=1)

    def back(m, picked):
        count, plus, minus, w_ref = ((ONE, AT_P1, AT_N1, w1_ref), (TWO, AT_P2, AT_N2, w2_ref))[m]
        gp, gn = dconv(plus, count), dconv(minus, count)
        for at, width in chunks(count)[picked]:
            c, s = wide(trig_s[2 * m], width), wide(trig_s[2 * m + 1], width)
            left, right = w_ref[cols(at, width), cols(0, count)], w_ref[cols(at, width), cols(count, count)]
            back_p = dot_t(gp, left) + dot_t(gn, right)
            back_n = dot_t(gn, left) - dot_t(gp, right)
            scatter(plus + at, width, c * back_p + s * back_n)
            scatter(minus + at, width, c * back_n - s * back_p)


    dz = dconv(AT_Z, ZERO)
    for at, width in chunks(ZERO):
        scatter(at, width, dot_t(dz, w0_ref[cols(at, width), :]))
    @pl.when(core == 0)
    def _():
        for k, span in enumerate(SHARES[0]):
            share_copy(k, span).wait_recv()
        for j in range(3):
            dp_, dn_ = pair(AT_P1 + 2 * j, 2), pair(AT_N1 + 2 * j, 2)
            rp, rn = factor(AT_P1, ONE), factor(AT_N1, ONE)
            put_aligned(dot(rp, dp_) + dot(rn, dn_), (2 * j, 2 * j + 1))
            put_aligned(dot(rp, dn_) - dot(rn, dp_), (6 + 2 * j, 7 + 2 * j))
            ready(12 * j, 12 * j + 12)
        two_blocks(0, 0, 2)
        ready(36, 48)
        for k, span in enumerate(SHARES[1]):
            share_copy(k, span).wait_send()

    @pl.when(core == 1)
    def _():
        for k, span in enumerate(SHARES[1]):
            share_copy(k, span).wait_recv()
        blank = jnp.zeros((NZ, 8, LANES), F32)
        for row_y in range(NY):
            for at in (46, 47):
                part2[row_y, spot(at)[1], :, spot(at)[2]] = blank
        for at, width in chunks(ZERO):
            put_shifted(1, 0, 4, 28, dot(factor(AT_Z, ZERO), pair(AT_Z + at, width)), range(at, at + width))
            ready(4 * at, 4 * (at + width))
        two_blocks(1, 2, 2)
        two_blocks(1, 4, 1)
        ready(28, 48)
        for k, span in enumerate(SHARES[0]):
            share_copy(k, span).wait_send()

    back(0, slice(0, 1))
    advance(0, 0, 1)
    back(0, slice(1, 3))
    advance(0, 0, 2)
    advance(1, 0, 1)
    advance(2, 0, 1)
    back(1, slice(0, 1))
    advance(0, 0, 3)
    back(1, slice(1, 3))
    node_up.start()
    node_down.start()
    finish(0, 0, s20)
    begin(0, 1)
    finish(1, 0, s21)
    begin(1, 1)
    finish(2, 0, s22)
    begin(2, 1)
    advance(0, 1, 1)
    advance(1, 1, 1)
    advance(2, 1, 1)
    finish(0, 1, s30)
    last_begin(0)
    finish(1, 1, s31)
    last_begin(1)
    finish(2, 1, s32)
    last_begin(2)
    last_end(0)
    node_up.wait()
    node_down.wait()
    nodes_out[pl.ds(0, 8)] = (node_ref[pl.ds(8, 8)] + node_in[0]).astype(BF16)
    nodes_out[pl.ds(8, 8)] = (node_ref[pl.ds(16, 8)] + node_in[1]).astype(BF16)
    last_end(1)
    last_end(2)
    for part in range(3):
        for stage in range(2):
            sent(part, stage)
        for offset in range(1, COUNT[AXES[part][2]]):
            last_copy(part, offset).wait_send()
    for part in range(3):
        for offset in range(1, 8):
            all_copy(part, offset).wait_recv()
    tiles_out[...] = gathered[...] * 0.125
    for part in range(3):
        for offset in range(1, 8):
            all_copy(part, offset).wait_send()
    for k in range(3):
        for copy in halo_copies(k):
            copy.wait_send()


def place_kernel(tiles_ref, nodes_ref, nodes_out, zero_out, one_out, two_out):
    nodes_out[...] = nodes_ref[...]
    outs = (zero_out, one_out, two_out)
    for which in range(2):
        for at, (matrix, i, b) in enumerate(TILES[which]):
            part, px, pk = spot(at)
            out = outs[matrix]
            rows = min(8, out.shape[0] - 8 * i)
            out[pl.ds(8 * i, rows), cols(b)] = tiles_ref[px * 2 + which, FIRST_OF[part] + pk, pl.ds(0, rows)]


def shards(node_feats, node_cotan, source, target, angle, w_zero, w_one, w_two):
    width = node_feats.shape[2]
    vmem = pl.BlockSpec(memory_space=pltpu.VMEM)
    hbm = pl.BlockSpec(memory_space=pl.ANY)
    dims = [[COUNT[a] for a in axes] for axes in AXES]
    tile = [(k, 8, LANES) for k in TILES_OF]

    def ring(part, stage):
        n = dims[part][stage]
        inner = dims[part][stage + 1 :]
        return pltpu.VMEM((2 * (n - 1), inner[0] // 2, *inner[1:], *tile[part]), F32)

    def leaf(part):
        pairs = dims[part][1] // 2 * dims[part][2] * TILES_OF[part] // 2
        return pltpu.VMEM((4, pairs, 16, LANES), BF16)

    dma = pltpu.SemaphoreType.DMA
    nodes, tiles = pl.pallas_call(
        edge_kernel,
        out_shape=(
            jax.ShapeDtypeStruct((16, width), BF16),
            jax.ShapeDtypeStruct((8, 12, 8, LANES), F32),
        ),
        in_specs=[vmem] * 5 + [hbm] * 3,
        out_specs=(vmem,) * 2,
        scratch_shapes=[
            pltpu.VMEM(w_zero.shape, BF16),
            pltpu.VMEM(w_one.shape, BF16),
            pltpu.VMEM(w_two.shape, BF16),
            pltpu.VMEM((64, width), BF16),
            pltpu.VMEM((EDGES, width), BF16),
            pltpu.VMEM((EDGES, width), F32),
            pltpu.VMEM((4, EDGES, LANES), F32),
            pltpu.VMEM((2, EDGES, LANES), BF16),
            pltpu.VMEM((32, width), F32),
            pltpu.VMEM((BLOCKS, LANES, 2 * PADDED), BF16),
            pltpu.VMEM((BLOCKS, 2 * PADDED, LANES), BF16),
            *[pltpu.VMEM((*dims[p], *tile[p]), F32) for p in range(3)],
            *[ring(p, 0) for p in range(3)],
            *[pltpu.VMEM((*dims[p][1:], *tile[p]), F32) for p in range(3)],
            *[ring(p, 1) for p in range(3)],
            *[pltpu.VMEM((dims[p][2], *tile[p]), F32) for p in range(3)],
            *[pltpu.VMEM((dims[p][2] - 1, *tile[p]), F32) for p in range(3)],
            *[leaf(p) for p in range(3)],
            *[leaf(p) for p in range(3)],
            pltpu.VMEM((8, 12, 8, LANES), F32),
            pltpu.VMEM((NZ, 120, 2 * LANES), F32),
            pltpu.VMEM((2, 8, width), F32),
            dma((3,)), dma((5,)), dma((5,)),
            dma((3, 14)), dma((3, 14)), dma((3, 14)), dma((3, 14)), dma((3, 7)), dma((3, 7)),
            dma((3, 7)), dma((3, 7)), dma((2,)), dma((2,)), dma((3, 2)), dma((3, 2)),
        ],
        compiler_params=pltpu.CompilerParams(
            vmem_limit_bytes=VMEM_LIMIT, collective_id=0, has_side_effects=True
        ),
        name="edge_gradients",
    )(node_feats[0], node_cotan[0], source, target, angle, w_zero, w_one, w_two)
    nodes, zero_g, one_g, two_g = pl.pallas_call(
        place_kernel,
        out_shape=(
            jax.ShapeDtypeStruct((16, width), BF16),
            jax.ShapeDtypeStruct((28, ZERO * LANES), F32),
            jax.ShapeDtypeStruct((24, 2 * ONE * LANES), F32),
            jax.ShapeDtypeStruct((20, 2 * TWO * LANES), F32),
        ),
        in_specs=[vmem] * 2,
        out_specs=(vmem,) * 4,
        name="place_tiles",
    )(tiles, nodes)
    return nodes[None], zero_g, one_g, two_g


def solution(mesh):
    placed = (
        P("dp", "graph", None),
        P("dp", "graph", None),
        P("dp", "graph"),
        P("dp", "graph"),
        P("dp", "graph"),
        P(),
        P(),
        P(),
    )
    return jax.shard_map(
        shards,
        mesh=mesh,
        in_specs=placed,
        out_specs=(P("dp", "graph", None), P("graph", None), P("graph", None), P("graph", None)),
        check_vma=False,
    )
```

```python
import jax
import jax.numpy as jnp
from jax import lax
from jax.experimental import pallas as pl
from jax.experimental.pallas import tpu as pltpu
from jax.sharding import PartitionSpec as P

MESH = pl.DeviceIdType.MESH
F32 = jnp.float32
BF16 = jnp.bfloat16
HEADS = 8
LANES = 128
EDGES = 320
PADDED = 384
BLOCKS = 29
ZERO, ONE, TWO = 7, 6, 5
AT_Z, AT_P1, AT_N1, AT_P2, AT_N2 = 0, 7, 13, 19, 24
VMEM_LIMIT = 62 * 1024 * 1024


def dot(a, b):
    return jnp.dot(a, b, preferred_element_type=F32)


def dot_t(a, b):
    return lax.dot_general(a, b, (((1,), (1,)), ((), ())), preferred_element_type=F32)


def dot_first(a, b):
    return lax.dot_general(a, b, (((0,), (0,)), ((), ())), preferred_element_type=F32)


def split2(v):
    high = v.astype(BF16)
    return high, (v - high.astype(F32)).astype(BF16)


def split3(v):
    high = v.astype(BF16)
    rest = v - high.astype(F32)
    middle = rest.astype(BF16)
    return high, middle, (rest - middle.astype(F32)).astype(BF16)


def chunks(count):
    out, at = [], 0
    while at < count:
        width = min(2, count - at)
        out.append((at, width))
        at += width
    return out


def cols(block, width=1):
    return pl.ds(block * LANES, width * LANES)


def wide(v, width):
    return v if width == 1 else jnp.concatenate([v] * width, axis=1)


def folded(v, width):
    return v if width == 1 else v[:, :LANES] + v[:, LANES:]


SHARES = (
    (
        (0, 7, 29), (1, 7, 9), (1, 13, 15), (1, 9, 11), (1, 15, 17), (1, 11, 13), (1, 17, 19),
        (1, 19, 21), (1, 24, 26),
    ),
    ((0, 0, 7), (0, 19, 29), (1, 0, 7), (1, 21, 24), (1, 26, 29)),
)
MADE = (
    7, 8, 13, 14, 0, 1, 2, 3, 4, 5, 6, 9, 10, 15, 16, 11, 12, 17, 18, 19, 20, 24, 25, 21, 22, 23, 26, 27, 28,
)
ONE_ORDER = tuple(b for j in range(3) for b in (2 * j, 2 * j + 1, 6 + 2 * j, 7 + 2 * j))
TILES = (
    tuple((1, i, b) for b in ONE_ORDER for i in range(3)) + tuple((2, i, b) for b in (0, 1, 5, 6) for i in range(3)),
    tuple((0, i, b) for b in range(7) for i in range(4)) + tuple((2, i, b) for b in (2, 3, 4, 7, 8, 9) for i in range(3)),
)
PLACE = tuple({tile: at for at, tile in enumerate(order)} for order in TILES)
NX, NY, NZ = 4, 4, 8
AXES = (("z", "x", "y"), ("x", "y", "z"), ("y", "x", "z"))
TILES_OF = (3, 4, 5)
FIRST_OF = (0, TILES_OF[0], TILES_OF[0] + TILES_OF[1])
COUNT = {"x": NX, "y": NY, "z": NZ}


def spot(at):
    part = 0 if at < 4 * FIRST_OF[1] else 1 if at < 4 * FIRST_OF[2] else 2
    inside = at - 4 * FIRST_OF[part]
    return part, inside // TILES_OF[part], inside % TILES_OF[part]


def chains_of(n):
    return ((1, 0, n // 2), (-1, 1, n // 2), (1, 1, n // 2 - 1), (-1, 0, n // 2 - 1))


def edge_kernel(
    feats_ref, cotan_ref, source_ref, target_ref, angle_ref, w0_hbm, w1_hbm, w2_hbm,
    nodes_out, tiles_out,
    w0_ref, w1_ref, w2_ref, tab_ref, x_s, du_s, trig_s, oh_s, node_ref,
    xt_s, d_s, part0, part1, part2, r10, r11, r12, s20, s21, s22, r20, r21, r22, s30, s31, s32, r30, r31, r32,
    o0, o1, o2, i0, i1, i2, gathered, result, node_in,
    load_sem, share_send, share_recv, send1, recv1, send2, recv2, send3, recv3, all_send, all_recv, node_send, node_recv,
    halo_send, halo_recv,
):
    dp = lax.axis_index("dp")
    graph = lax.axis_index("graph")
    core, x = dp % 2, dp // 2
    y, z = graph % NY, graph // NY
    place = {"x": x, "y": y, "z": z}

    def moved(axis, offset):
        n = COUNT[axis]
        to = (place[axis] + offset + n) % n
        if axis == "x":
            return {"dp": to * 2 + core, "graph": graph}
        if axis == "y":
            return {"dp": dp, "graph": z * NY + to}
        return {"dp": dp, "graph": to * NY + y}

    sibling = {"dp": x * 2 + (1 - core), "graph": graph}
    graphs = NY * NZ
    before = {"dp": dp, "graph": (graph + graphs - 1) % graphs}
    after = {"dp": dp, "graph": (graph + 1) % graphs}
    peers = [{"dp": (dp + o) % 8, "graph": graph} for o in range(1, 8)]
    peers += [moved("y", o) for o in range(1, NY)] + [moved("z", o) for o in range(1, NZ)] + [before, after]

    barrier = pltpu.get_barrier_semaphore()
    for peer in peers:
        pl.semaphore_signal(barrier, inc=1, device_id=peer, device_id_type=MESH)
    loads = [
        pltpu.make_async_copy(src, dst, load_sem.at[k])
        for k, (src, dst) in enumerate(((w0_hbm, w0_ref), (w1_hbm, w1_ref), (w2_hbm, w2_ref)))
    ]
    for load in loads:
        load.start()
    feats, cotan = feats_ref[...].astype(F32), cotan_ref[...].astype(F32)
    tab_ref[pl.ds(0, 16)] = jnp.concatenate([feats[:8], cotan[:8]], 0).astype(BF16)
    tab_ref[pl.ds(16, 16)] = jnp.concatenate([feats[8:], cotan[8:]], 0).astype(BF16)
    def remote(src, dst, send, recv, device):
        return pltpu.make_async_remote_copy(
            src_ref=src, dst_ref=dst, send_sem=send, recv_sem=recv, device_id=device, device_id_type=MESH
        )

    node_up = remote(node_ref.at[pl.ds(0, 8)], node_in.at[1], node_send.at[0], node_recv.at[0], before)
    node_down = remote(node_ref.at[pl.ds(24, 8)], node_in.at[0], node_send.at[1], node_recv.at[1], after)

    def own_half(kind, lo, hi, half):
        if kind == 0:
            return xt_s.at[pl.ds(lo, hi - lo), :, pl.ds(half * PADDED, PADDED)]
        return d_s.at[pl.ds(lo, hi - lo), pl.ds(half * PADDED, PADDED), :]

    def share_copy(k, span):
        return remote(own_half(*span, 0), own_half(*span, 1), share_send.at[k], share_recv.at[k], sibling)

    stage1 = (part0, part1, part2)
    rings1 = (r10, r11, r12)
    stage2 = (s20, s21, s22)
    rings2 = (r20, r21, r22)
    stage3 = (s30, s31, s32)
    slots3 = (r30, r31, r32)

    outs16, ins16 = (o0, o1, o2), (i0, i1, i2)

    def slot_of(n, chain, step):
        return sum(c[2] for c in chains_of(n)[:chain]) + step

    def ring_copy(part, stage, chain, step):
        axis = AXES[part][stage]
        n = COUNT[axis]
        way, half, steps = chains_of(n)[chain]
        source, ring = ((stage1, rings1), (stage2, rings2))[stage]
        sends, recvs = ((send1, recv1), (send2, recv2))[stage]
        deep = source[part].shape[1] // 2
        slot = slot_of(n, chain, step)
        if step == 0 and stage == 0:
            return remote(
                outs16[part].at[chain], ins16[part].at[chain],
                sends.at[part, slot], recvs.at[part, slot], moved(axis, way),
            )
        if step == 0:
            block = (place[axis] + way * steps + n) % n
            src = source[part].at[block, pl.ds(half * deep, deep)]
        else:
            src = ring[part].at[slot - 1]
        return remote(src, ring[part].at[slot], sends.at[part, slot], recvs.at[part, slot], moved(axis, way))

    def begin(part, stage, picked=(0, 1, 2, 3)):
        axis = AXES[part][stage]
        n = COUNT[axis]
        for chain in picked:
            way, half, steps = chains_of(n)[chain]
            if stage == 0:
                deep = stage1[part].shape[1] // 2
                block = (place[axis] + way * steps + n) % n
                v = stage1[part][block, pl.ds(half * deep, deep)]
                outs16[part][chain] = v.reshape(outs16[part].shape[1:]).astype(BF16)
            ring_copy(part, stage, chain, 0).start()

    def arrival(part, stage, chain, step):
        n = COUNT[AXES[part][stage]]
        ring = (rings1, rings2)[stage][part]
        if stage == 0 and step == 0:
            return ins16[part][chain].astype(F32).reshape(ring.shape[1:])
        return ring[slot_of(n, chain, step)]

    def advance(part, stage, step, picked=(0, 1, 2, 3)):
        axis = AXES[part][stage]
        n = COUNT[axis]
        source, ring = ((stage1, rings1), (stage2, rings2))[stage]
        deep = source[part].shape[1] // 2
        for chain, (way, half, steps) in enumerate(chains_of(n)):
            if step < steps and chain in picked:
                slot = slot_of(n, chain, step)
                ring_copy(part, stage, chain, step - 1).wait_recv()
                block = (place[axis] + way * (steps - step) + n) % n
                ring[part][slot - 1] = arrival(part, stage, chain, step - 1) + source[part][block, pl.ds(half * deep, deep)]
                ring_copy(part, stage, chain, step).start()

    def finish(part, stage, out):
        axis = AXES[part][stage]
        n = COUNT[axis]
        source, ring = ((stage1, rings1), (stage2, rings2))[stage]
        deep = source[part].shape[1] // 2
        for half in range(2):
            arrived = []
            for chain, (way, h, steps) in enumerate(chains_of(n)):
                if h == half:
                    ring_copy(part, stage, chain, steps - 1).wait_recv()
                    arrived.append(arrival(part, stage, chain, steps - 1))
            out[pl.ds(half * deep, deep)] = source[part][place[axis], pl.ds(half * deep, deep)] + arrived[0] + arrived[1]

    def sent(part, stage):
        for chain, (way, half, steps) in enumerate(chains_of(COUNT[AXES[part][stage]])):
            for step in range(steps):
                ring_copy(part, stage, chain, step).wait_send()

    def last_copy(part, offset):
        axis = AXES[part][2]
        n = COUNT[axis]
        return remote(
            stage3[part].at[(place[axis] + offset) % n], slots3[part].at[offset - 1],
            send3.at[part, offset - 1], recv3.at[part, offset - 1], moved(axis, offset),
        )

    def last_begin(part):
        for offset in range(1, COUNT[AXES[part][2]]):
            last_copy(part, offset).start()

    def all_copy(part, offset):
        mine = gathered.at[dp, pl.ds(FIRST_OF[part], TILES_OF[part])]
        return remote(
            mine, mine, all_send.at[part, offset - 1], all_recv.at[part, offset - 1],
            {"dp": (dp + offset) % 8, "graph": graph},
        )

    def last_end(part):
        axis = AXES[part][2]
        whole = stage3[part][place[axis]]
        for offset in range(1, COUNT[axis]):
            last_copy(part, offset).wait_recv()
            whole = whole + slots3[part][offset - 1]
        gathered[dp, pl.ds(FIRST_OF[part], TILES_OF[part])] = whole
        for offset in range(1, 8):
            all_copy(part, offset).start()

    def ready(had, have):
        for part in range(3):
            if had < 4 * (FIRST_OF[part] + TILES_OF[part]) <= have:
                begin(part, 0, (0, 1))

    def put(which, tile, row_y, v):
        at = PLACE[which][tile]
        part, px, pk = spot(at)
        if part == 0:
            part0[:, px, row_y, pk] = v
        elif part == 1:
            part1[px, row_y, :, pk] = v
        else:
            part2[row_y, px, :, pk] = v

    def pair(block, width):
        return jnp.concatenate([d_s[block + k] for k in range(width)], axis=1)

    def factor(block, count):
        return xt_s[pl.ds(block, count)].reshape(count * LANES, 2 * PADDED)

    def put_aligned(v, first_blocks):
        shaped = v.reshape(NZ, NY * 3, 8, v.shape[1])
        for w, b in enumerate(first_blocks):
            for row_y in range(NY):
                for i in range(3):
                    put(0, (1, i, b), row_y, shaped[:, row_y * 3 + i, :, w * LANES : (w + 1) * LANES])

    def put_shifted(which, matrix, tiles, shard, v, first_blocks):
        result[:, pl.ds(0, NY * shard), pl.ds(0, v.shape[1])] = v.reshape(NZ, NY * shard, v.shape[1])
        for w, b in enumerate(first_blocks):
            for row_y in range(NY):
                for i in range(tiles):
                    put(which, (matrix, i, b), row_y, result[:, pl.ds(row_y * shard + i * 8, 8), cols(w)])

    def two_blocks(which, at, width):
        dp_, dn_ = pair(AT_P2 + at, width), pair(AT_N2 + at, width)
        rp, rn = factor(AT_P2, TWO), factor(AT_N2, TWO)
        put_shifted(which, 2, 3, 20, dot(rp, dp_) + dot(rn, dn_), range(at, at + width))
        put_shifted(which, 2, 3, 20, dot(rp, dn_) - dot(rn, dp_), range(TWO + at, TWO + at + width))


    orders = ((0, AT_P1), (AT_P1, AT_P2), (AT_P2, BLOCKS))

    def halo_copies(k):
        span = pl.ds(orders[k][0] * LANES, (orders[k][1] - orders[k][0]) * LANES)
        return (
            remote(
                tab_ref.at[pl.ds(16, 16), span], tab_ref.at[pl.ds(32, 16), span],
                halo_send.at[k, 0], halo_recv.at[k, 0], after,
            ),
            remote(
                tab_ref.at[pl.ds(0, 16), span], tab_ref.at[pl.ds(48, 16), span],
                halo_send.at[k, 1], halo_recv.at[k, 1], before,
            ),
        )

    first_atom = graph * 16 - 8

    def table_row(atoms, shift):
        local = atoms - first_atom
        block = local >> 3
        base = jnp.where(block == 0, 32, jnp.where(block == 1, 0, jnp.where(block == 2, 16, 48)))
        return (base + (local & 7) + shift).astype(F32)

    row = lax.broadcasted_iota(jnp.int32, (8, EDGES), 0)
    phases = jnp.broadcast_to(angle_ref[...], (8, EDGES))
    phases = jnp.where(row < 2, phases, 2.0 * phases)
    ends = jnp.where(row == 4, table_row(source_ref[...], 0), table_row(target_ref[...], 8))
    rows = jnp.where(row >= 4, ends, jnp.where((row & 1) == 0, jnp.cos(phases), jnp.sin(phases)))
    parts = jnp.concatenate(list(split3(rows)), axis=0)
    pick_row = lax.broadcasted_iota(jnp.int32, (24, 6 * LANES), 0)
    pick_col = lax.broadcasted_iota(jnp.int32, (24, 6 * LANES), 1)
    chosen = jnp.where(pick_row % 8 == pick_col // LANES, 1.0, 0.0).astype(BF16)
    spread = dot_first(parts, chosen)
    for k in range(4):
        trig_s[k] = spread[:, k * LANES : (k + 1) * LANES]
    lane = lax.broadcasted_iota(jnp.int32, (EDGES, LANES), 1).astype(F32)
    for k in range(2):
        oh_s[k] = jnp.where(spread[:, (4 + k) * LANES : (5 + k) * LANES] == lane, 1.0, 0.0).astype(BF16)
    depth = tab_ref.shape[0]
    oh_src = oh_s[0, :, :depth]
    oh_dst = oh_s[1, :, :depth]

    pl.semaphore_wait(barrier, len(peers))

    for k in range(3):
        for copy in halo_copies(k):
            copy.start()
    xt_s[:, :, EDGES:PADDED] = jnp.zeros((BLOCKS, LANES, PADDED - EDGES), BF16)
    d_s[:, EDGES:PADDED, :] = jnp.zeros((BLOCKS, PADDED - EDGES, LANES), BF16)
    result[...] = jnp.zeros_like(result)

    def keep_x(block, width, v):
        x_s[:, cols(block, width)] = v
        for w in range(width):
            xt_s[block + w, :, :EDGES] = v[:, w * LANES : (w + 1) * LANES].T

    def rotated(onehot, c, s, plus, minus, width):
        a = dot(onehot, tab_ref[:, cols(plus, width)])
        b = dot(onehot, tab_ref[:, cols(minus, width)])
        return c * a - s * b, s * a + c * b

    for copy in halo_copies(0):
        copy.wait_recv()
    for at, width in chunks(ZERO):
        keep_x(at, width, dot(oh_src, tab_ref[:, cols(at, width)]).astype(BF16))
    for m, (count, plus, minus) in enumerate(((ONE, AT_P1, AT_N1), (TWO, AT_P2, AT_N2))):
        for copy in halo_copies(1 + m):
            copy.wait_recv()
        for at, width in chunks(count):
            c, s = wide(trig_s[2 * m], width), wide(trig_s[2 * m + 1], width)
            p, n = rotated(oh_src, c, s, plus + at, minus + at, width)
            keep_x(plus + at, width, p.astype(BF16))
            keep_x(minus + at, width, n.astype(BF16))


    def share(chosen):
        for other in range(2):
            spans = [k for k, span in enumerate(SHARES[other]) if chosen(*span)]
            if spans:
                @pl.when(core == 1 - other)
                def _(other=other, spans=spans):
                    for k in spans:
                        share_copy(k, SHARES[other][k]).start()

    share(lambda kind, lo, hi: kind == 0)
    for load in loads:
        load.wait()
    total = jnp.zeros((EDGES, LANES), F32)
    first = None
    for at, width in chunks(ZERO):
        out = dot(x_s[:, cols(0, ZERO)], w0_ref[:, cols(at, width)])
        if at == 0:
            first = out[:, :LANES]
        up = dot(oh_dst, tab_ref[:, cols(at, width)])
        du_s[:, cols(at, width)] = up
        total = total + folded(up * out, width)
    for m, (count, plus, minus, w_ref) in enumerate(((ONE, AT_P1, AT_N1, w1_ref), (TWO, AT_P2, AT_N2, w2_ref))):
        for at, width in chunks(count):
            c, s = wide(trig_s[2 * m], width), wide(trig_s[2 * m + 1], width)
            up_p, up_n = rotated(oh_dst, c, s, plus + at, minus + at, width)
            du_s[:, cols(plus + at, width)] = up_p
            du_s[:, cols(minus + at, width)] = up_n
            xp, xn = x_s[:, cols(plus, count)], x_s[:, cols(minus, count)]
            left, right = w_ref[:, cols(at, width)], w_ref[:, cols(count + at, width)]
            out_p = dot(xp, left) - dot(xn, right)
            out_n = dot(xp, right) + dot(xn, left)
            total = total + folded(up_p * out_p + up_n * out_n, width)

    size = LANES // HEADS
    head_r = lax.broadcasted_iota(jnp.int32, (LANES, LANES), 0) // size
    head_c = lax.broadcasted_iota(jnp.int32, (LANES, LANES), 1) // size
    same = jnp.where(head_r == head_c, 1.0, 0.0).astype(BF16)

    def head_sum(v):
        high, middle, low = split3(v)
        return dot(low, same) + dot(middle, same) + dot(high, same)

    scale = 1.0 / (float(size) ** 0.5)
    gate = jax.nn.sigmoid(head_sum(first) * scale)
    dlogit = head_sum(total) * gate * (1.0 - gate) * scale
    for block in MADE:
        v = du_s[:, cols(block)] * gate
        if block == 0:
            v = v + dlogit
        d_s[block, :EDGES, :] = v.astype(BF16)
        share(lambda kind, lo, hi: kind == 1 and block + 1 == hi)


    atoms = node_ref.shape[0]
    atom = lax.broadcasted_iota(jnp.int32, (atoms, EDGES), 0)
    table_row = jnp.where(atom < 8, atom + 32, jnp.where(atom < 16, atom - 8, jnp.where(atom < 24, atom, atom + 24)))
    oh_rows = jnp.where(table_row.astype(F32) == rows[4:5, :], 1.0, 0.0).astype(BF16)

    def scatter(block, width, v):
        high, low = split2(v)
        node_ref[:, cols(block, width)] = dot(oh_rows, high) + dot(oh_rows, low)

    def dconv(block, count):
        return jnp.concatenate([d_s[block + k, :EDGES, :] for k in range(count)], axis=1)

    def back(m, picked):
        count, plus, minus, w_ref = ((ONE, AT_P1, AT_N1, w1_ref), (TWO, AT_P2, AT_N2, w2_ref))[m]
        gp, gn = dconv(plus, count), dconv(minus, count)
        for at, width in chunks(count)[picked]:
            c, s = wide(trig_s[2 * m], width), wide(trig_s[2 * m + 1], width)
            left, right = w_ref[cols(at, width), cols(0, count)], w_ref[cols(at, width), cols(count, count)]
            back_p = dot_t(gp, left) + dot_t(gn, right)
            back_n = dot_t(gn, left) - dot_t(gp, right)
            scatter(plus + at, width, c * back_p + s * back_n)
            scatter(minus + at, width, c * back_n - s * back_p)


    dz = dconv(AT_Z, ZERO)
    for at, width in chunks(ZERO):
        scatter(at, width, dot_t(dz, w0_ref[cols(at, width), :]))
    @pl.when(core == 0)
    def _():
        share_copy(0, SHARES[0][0]).wait_recv()
        for j in range(3):
            for k in (1 + 2 * j, 2 + 2 * j):
                share_copy(k, SHARES[0][k]).wait_recv()
            dp_, dn_ = pair(AT_P1 + 2 * j, 2), pair(AT_N1 + 2 * j, 2)
            rp, rn = factor(AT_P1, ONE), factor(AT_N1, ONE)
            put_aligned(dot(rp, dp_) + dot(rn, dn_), (2 * j, 2 * j + 1))
            put_aligned(dot(rp, dn_) - dot(rn, dp_), (6 + 2 * j, 7 + 2 * j))
            ready(12 * j, 12 * j + 12)
        for k in (7, 8):
            share_copy(k, SHARES[0][k]).wait_recv()
        two_blocks(0, 0, 2)
        ready(36, 48)
        for k, span in enumerate(SHARES[1]):
            share_copy(k, span).wait_send()

    @pl.when(core == 1)
    def _():
        for k in (0, 2):
            share_copy(k, SHARES[1][k]).wait_recv()
        blank = jnp.zeros((NZ, 8, LANES), F32)
        for row_y in range(NY):
            for at in (46, 47):
                part2[row_y, spot(at)[1], :, spot(at)[2]] = blank
        for at, width in chunks(ZERO):
            put_shifted(1, 0, 4, 28, dot(factor(AT_Z, ZERO), pair(AT_Z + at, width)), range(at, at + width))
            ready(4 * at, 4 * (at + width))
        for k in (1, 3, 4):
            share_copy(k, SHARES[1][k]).wait_recv()
        two_blocks(1, 2, 2)
        two_blocks(1, 4, 1)
        ready(28, 48)
        for k, span in enumerate(SHARES[0]):
            share_copy(k, span).wait_send()

    begin(0, 0, (2, 3))
    advance(0, 0, 1, (0, 1))
    begin(1, 0, (2, 3))
    begin(2, 0, (2, 3))
    advance(0, 0, 1, (2, 3))
    back(0, slice(0, 1))
    advance(1, 0, 1)
    advance(2, 0, 1)
    advance(0, 0, 2, (0, 1))
    advance(0, 0, 2, (2, 3))
    back(0, slice(1, 2))
    advance(0, 0, 3)
    back(0, slice(2, 3))
    finish(1, 0, s21)
    begin(1, 1)
    finish(0, 0, s20)
    begin(0, 1)
    finish(2, 0, s22)
    begin(2, 1)
    back(1, slice(0, 1))
    advance(1, 1, 1)
    advance(0, 1, 1)
    advance(2, 1, 1)
    back(1, slice(1, 2))
    finish(1, 1, s31)
    last_begin(1)
    finish(0, 1, s30)
    last_begin(0)
    finish(2, 1, s32)
    last_begin(2)
    back(1, slice(2, 3))
    node_up.start()
    node_down.start()
    last_end(0)
    last_end(1)
    last_end(2)
    node_up.wait()
    node_down.wait()
    nodes_out[pl.ds(0, 8)] = (node_ref[pl.ds(8, 8)] + node_in[0]).astype(BF16)
    nodes_out[pl.ds(8, 8)] = (node_ref[pl.ds(16, 8)] + node_in[1]).astype(BF16)
    for part in range(3):
        for stage in range(2):
            sent(part, stage)
        for offset in range(1, COUNT[AXES[part][2]]):
            last_copy(part, offset).wait_send()
    for part in range(3):
        for offset in range(1, 8):
            all_copy(part, offset).wait_recv()
    tiles_out[...] = gathered[...] * 0.125
    for part in range(3):
        for offset in range(1, 8):
            all_copy(part, offset).wait_send()
    for k in range(3):
        for copy in halo_copies(k):
            copy.wait_send()


def place_kernel(tiles_ref, nodes_ref, nodes_out, zero_out, one_out, two_out):
    nodes_out[...] = nodes_ref[...]
    outs = (zero_out, one_out, two_out)
    for which in range(2):
        for at, (matrix, i, b) in enumerate(TILES[which]):
            part, px, pk = spot(at)
            out = outs[matrix]
            rows = min(8, out.shape[0] - 8 * i)
            out[pl.ds(8 * i, rows), cols(b)] = tiles_ref[px * 2 + which, FIRST_OF[part] + pk, pl.ds(0, rows)]


def shards(node_feats, node_cotan, source, target, angle, w_zero, w_one, w_two):
    width = node_feats.shape[2]
    vmem = pl.BlockSpec(memory_space=pltpu.VMEM)
    hbm = pl.BlockSpec(memory_space=pl.ANY)
    dims = [[COUNT[a] for a in axes] for axes in AXES]
    tile = [(k, 8, LANES) for k in TILES_OF]

    def ring(part, stage):
        n = dims[part][stage]
        inner = dims[part][stage + 1 :]
        return pltpu.VMEM((2 * (n - 1), inner[0] // 2, *inner[1:], *tile[part]), F32)

    def leaf(part):
        pairs = dims[part][1] // 2 * dims[part][2] * TILES_OF[part] // 2
        return pltpu.VMEM((4, pairs, 16, LANES), BF16)

    dma = pltpu.SemaphoreType.DMA
    nodes, tiles = pl.pallas_call(
        edge_kernel,
        out_shape=(
            jax.ShapeDtypeStruct((16, width), BF16),
            jax.ShapeDtypeStruct((8, 12, 8, LANES), F32),
        ),
        in_specs=[vmem] * 5 + [hbm] * 3,
        out_specs=(vmem,) * 2,
        scratch_shapes=[
            pltpu.VMEM(w_zero.shape, BF16),
            pltpu.VMEM(w_one.shape, BF16),
            pltpu.VMEM(w_two.shape, BF16),
            pltpu.VMEM((64, width), BF16),
            pltpu.VMEM((EDGES, width), BF16),
            pltpu.VMEM((EDGES, width), F32),
            pltpu.VMEM((4, EDGES, LANES), F32),
            pltpu.VMEM((2, EDGES, LANES), BF16),
            pltpu.VMEM((32, width), F32),
            pltpu.VMEM((BLOCKS, LANES, 2 * PADDED), BF16),
            pltpu.VMEM((BLOCKS, 2 * PADDED, LANES), BF16),
            *[pltpu.VMEM((*dims[p], *tile[p]), F32) for p in range(3)],
            *[ring(p, 0) for p in range(3)],
            *[pltpu.VMEM((*dims[p][1:], *tile[p]), F32) for p in range(3)],
            *[ring(p, 1) for p in range(3)],
            *[pltpu.VMEM((dims[p][2], *tile[p]), F32) for p in range(3)],
            *[pltpu.VMEM((dims[p][2] - 1, *tile[p]), F32) for p in range(3)],
            *[leaf(p) for p in range(3)],
            *[leaf(p) for p in range(3)],
            pltpu.VMEM((8, 12, 8, LANES), F32),
            pltpu.VMEM((NZ, 120, 2 * LANES), F32),
            pltpu.VMEM((2, 8, width), F32),
            dma((3,)), dma((9,)), dma((9,)),
            dma((3, 14)), dma((3, 14)), dma((3, 14)), dma((3, 14)), dma((3, 7)), dma((3, 7)),
            dma((3, 7)), dma((3, 7)), dma((2,)), dma((2,)), dma((3, 2)), dma((3, 2)),
        ],
        compiler_params=pltpu.CompilerParams(
            vmem_limit_bytes=VMEM_LIMIT, collective_id=0, has_side_effects=True
        ),
        name="edge_gradients",
    )(node_feats[0], node_cotan[0], source, target, angle, w_zero, w_one, w_two)
    nodes, zero_g, one_g, two_g = pl.pallas_call(
        place_kernel,
        out_shape=(
            jax.ShapeDtypeStruct((16, width), BF16),
            jax.ShapeDtypeStruct((28, ZERO * LANES), F32),
            jax.ShapeDtypeStruct((24, 2 * ONE * LANES), F32),
            jax.ShapeDtypeStruct((20, 2 * TWO * LANES), F32),
        ),
        in_specs=[vmem] * 2,
        out_specs=(vmem,) * 4,
        name="place_tiles",
    )(tiles, nodes)
    return nodes[None], zero_g, one_g, two_g


def solution(mesh):
    placed = (
        P("dp", "graph", None),
        P("dp", "graph", None),
        P("dp", "graph"),
        P("dp", "graph"),
        P("dp", "graph"),
        P(),
        P(),
        P(),
    )
    return jax.shard_map(
        shards,
        mesh=mesh,
        in_specs=placed,
        out_specs=(P("dp", "graph", None), P("graph", None), P("graph", None), P("graph", None)),
        check_vma=False,
    )
```

```python
import jax
import jax.numpy as jnp
from jax import lax
from jax.experimental import pallas as pl
from jax.experimental.pallas import tpu as pltpu
from jax.sharding import PartitionSpec as P

MESH = pl.DeviceIdType.MESH
F32 = jnp.float32
BF16 = jnp.bfloat16
HEADS = 8
LANES = 128
EDGES = 320
PADDED = 384
BLOCKS = 29
ZERO, ONE, TWO = 7, 6, 5
AT_Z, AT_P1, AT_N1, AT_P2, AT_N2 = 0, 7, 13, 19, 24
VMEM_LIMIT = 62 * 1024 * 1024


def dot(a, b):
    return jnp.dot(a, b, preferred_element_type=F32)


def dot_t(a, b):
    return lax.dot_general(a, b, (((1,), (1,)), ((), ())), preferred_element_type=F32)


def dot_first(a, b):
    return lax.dot_general(a, b, (((0,), (0,)), ((), ())), preferred_element_type=F32)


def split2(v):
    high = v.astype(BF16)
    return high, (v - high.astype(F32)).astype(BF16)


def split3(v):
    high = v.astype(BF16)
    rest = v - high.astype(F32)
    middle = rest.astype(BF16)
    return high, middle, (rest - middle.astype(F32)).astype(BF16)


def chunks(count):
    out, at = [], 0
    while at < count:
        width = min(2, count - at)
        out.append((at, width))
        at += width
    return out


def cols(block, width=1):
    return pl.ds(block * LANES, width * LANES)


def wide(v, width):
    return v if width == 1 else jnp.concatenate([v] * width, axis=1)


def folded(v, width):
    return v if width == 1 else v[:, :LANES] + v[:, LANES:]


SHARES = (
    (
        (0, 7, 29), (1, 7, 9), (1, 13, 15), (1, 9, 11), (1, 15, 17), (1, 11, 13), (1, 17, 19),
        (1, 19, 21), (1, 24, 26),
    ),
    ((0, 0, 7), (0, 19, 29), (1, 0, 7), (1, 21, 24), (1, 26, 29)),
)
MADE = (
    7, 8, 13, 14, 0, 1, 2, 3, 4, 5, 6, 9, 10, 15, 16, 11, 12, 17, 18, 19, 20, 24, 25, 21, 22, 23, 26, 27, 28,
)
ONE_ORDER = tuple(b for j in range(3) for b in (2 * j, 2 * j + 1, 6 + 2 * j, 7 + 2 * j))
TILES = (
    tuple((1, i, b) for b in ONE_ORDER for i in range(3)) + tuple((2, i, b) for b in (0, 1, 5, 6) for i in range(3)),
    tuple((0, i, b) for b in range(7) for i in range(4)) + tuple((2, i, b) for b in (2, 3, 4, 7, 8, 9) for i in range(3)),
)
PLACE = tuple({tile: at for at, tile in enumerate(order)} for order in TILES)
NX, NY, NZ = 4, 4, 8
AXES = (("z", "x", "y"), ("x", "y", "z"), ("y", "x", "z"))
TILES_OF = (3, 4, 5)
FIRST_OF = (0, TILES_OF[0], TILES_OF[0] + TILES_OF[1])
COUNT = {"x": NX, "y": NY, "z": NZ}


def spot(at):
    part = 0 if at < 4 * FIRST_OF[1] else 1 if at < 4 * FIRST_OF[2] else 2
    inside = at - 4 * FIRST_OF[part]
    return part, inside // TILES_OF[part], inside % TILES_OF[part]


def chains_of(n):
    return ((1, 0, n // 2), (-1, 1, n // 2), (1, 1, n // 2 - 1), (-1, 0, n // 2 - 1))


def edge_kernel(
    feats_ref, cotan_ref, source_ref, target_ref, angle_ref, w0_hbm, w1_hbm, w2_hbm,
    nodes_out, tiles_out,
    w0_ref, w1_ref, w2_ref, tab_ref, x_s, du_s, trig_s, oh_s, node_ref,
    xt_s, d_s, part0, part1, part2, r10, r11, r12, s20, s21, s22, r20, r21, r22, s30, s31, s32, r30, r31, r32,
    o0, o1, o2, i0, i1, i2, gathered, result, node_in,
    load_sem, share_send, share_recv, send1, recv1, send2, recv2, send3, recv3, all_send, all_recv, node_send, node_recv,
    halo_send, halo_recv,
):
    dp = lax.axis_index("dp")
    graph = lax.axis_index("graph")
    core, x = dp % 2, dp // 2
    y, z = graph % NY, graph // NY
    place = {"x": x, "y": y, "z": z}

    def moved(axis, offset):
        n = COUNT[axis]
        to = (place[axis] + offset + n) % n
        if axis == "x":
            return {"dp": to * 2 + core, "graph": graph}
        if axis == "y":
            return {"dp": dp, "graph": z * NY + to}
        return {"dp": dp, "graph": to * NY + y}

    sibling = {"dp": x * 2 + (1 - core), "graph": graph}
    graphs = NY * NZ
    before = {"dp": dp, "graph": (graph + graphs - 1) % graphs}
    after = {"dp": dp, "graph": (graph + 1) % graphs}
    peers = [{"dp": (dp + o) % 8, "graph": graph} for o in range(1, 8)]
    peers += [moved("y", o) for o in range(1, NY)] + [moved("z", o) for o in range(1, NZ)] + [before, after]

    barrier = pltpu.get_barrier_semaphore()
    for peer in peers:
        pl.semaphore_signal(barrier, inc=1, device_id=peer, device_id_type=MESH)
    loads = [
        pltpu.make_async_copy(src, dst, load_sem.at[k])
        for k, (src, dst) in enumerate(((w0_hbm, w0_ref), (w1_hbm, w1_ref), (w2_hbm, w2_ref)))
    ]
    for load in loads:
        load.start()
    feats, cotan = feats_ref[...].astype(F32), cotan_ref[...].astype(F32)
    tab_ref[pl.ds(0, 16)] = jnp.concatenate([feats[:8], cotan[:8]], 0).astype(BF16)
    tab_ref[pl.ds(16, 16)] = jnp.concatenate([feats[8:], cotan[8:]], 0).astype(BF16)
    def remote(src, dst, send, recv, device):
        return pltpu.make_async_remote_copy(
            src_ref=src, dst_ref=dst, send_sem=send, recv_sem=recv, device_id=device, device_id_type=MESH
        )

    node_up = remote(node_ref.at[pl.ds(0, 8)], node_in.at[1], node_send.at[0], node_recv.at[0], before)
    node_down = remote(node_ref.at[pl.ds(24, 8)], node_in.at[0], node_send.at[1], node_recv.at[1], after)

    def own_half(kind, lo, hi, half):
        if kind == 0:
            return xt_s.at[pl.ds(lo, hi - lo), :, pl.ds(half * PADDED, PADDED)]
        return d_s.at[pl.ds(lo, hi - lo), pl.ds(half * PADDED, PADDED), :]

    def share_copy(k, span):
        return remote(own_half(*span, 0), own_half(*span, 1), share_send.at[k], share_recv.at[k], sibling)

    stage1 = (part0, part1, part2)
    rings1 = (r10, r11, r12)
    stage2 = (s20, s21, s22)
    rings2 = (r20, r21, r22)
    stage3 = (s30, s31, s32)
    slots3 = (r30, r31, r32)

    outs16, ins16 = (o0, o1, o2), (i0, i1, i2)

    def slot_of(n, chain, step):
        return sum(c[2] for c in chains_of(n)[:chain]) + step

    def ring_copy(part, stage, chain, step):
        axis = AXES[part][stage]
        n = COUNT[axis]
        way, half, steps = chains_of(n)[chain]
        source, ring = ((stage1, rings1), (stage2, rings2))[stage]
        sends, recvs = ((send1, recv1), (send2, recv2))[stage]
        deep = source[part].shape[1] // 2
        slot = slot_of(n, chain, step)
        if step == 0 and stage == 0:
            return remote(
                outs16[part].at[chain], ins16[part].at[chain],
                sends.at[part, slot], recvs.at[part, slot], moved(axis, way),
            )
        if step == 0:
            block = (place[axis] + way * steps + n) % n
            src = source[part].at[block, pl.ds(half * deep, deep)]
        else:
            src = ring[part].at[slot - 1]
        return remote(src, ring[part].at[slot], sends.at[part, slot], recvs.at[part, slot], moved(axis, way))

    def begin(part, stage, picked=(0, 1, 2, 3)):
        axis = AXES[part][stage]
        n = COUNT[axis]
        for chain in picked:
            way, half, steps = chains_of(n)[chain]
            if stage == 0:
                deep = stage1[part].shape[1] // 2
                block = (place[axis] + way * steps + n) % n
                v = stage1[part][block, pl.ds(half * deep, deep)]
                outs16[part][chain] = v.reshape(outs16[part].shape[1:]).astype(BF16)
            ring_copy(part, stage, chain, 0).start()

    def arrival(part, stage, chain, step):
        n = COUNT[AXES[part][stage]]
        ring = (rings1, rings2)[stage][part]
        if stage == 0 and step == 0:
            return ins16[part][chain].astype(F32).reshape(ring.shape[1:])
        return ring[slot_of(n, chain, step)]

    def advance(part, stage, step, picked=(0, 1, 2, 3)):
        axis = AXES[part][stage]
        n = COUNT[axis]
        source, ring = ((stage1, rings1), (stage2, rings2))[stage]
        deep = source[part].shape[1] // 2
        for chain, (way, half, steps) in enumerate(chains_of(n)):
            if step < steps and chain in picked:
                slot = slot_of(n, chain, step)
                ring_copy(part, stage, chain, step - 1).wait_recv()
                block = (place[axis] + way * (steps - step) + n) % n
                ring[part][slot - 1] = arrival(part, stage, chain, step - 1) + source[part][block, pl.ds(half * deep, deep)]
                ring_copy(part, stage, chain, step).start()

    def finish(part, stage, out):
        axis = AXES[part][stage]
        n = COUNT[axis]
        source, ring = ((stage1, rings1), (stage2, rings2))[stage]
        deep = source[part].shape[1] // 2
        for half in range(2):
            arrived = []
            for chain, (way, h, steps) in enumerate(chains_of(n)):
                if h == half:
                    ring_copy(part, stage, chain, steps - 1).wait_recv()
                    arrived.append(arrival(part, stage, chain, steps - 1))
            out[pl.ds(half * deep, deep)] = source[part][place[axis], pl.ds(half * deep, deep)] + arrived[0] + arrived[1]

    def sent(part, stage):
        for chain, (way, half, steps) in enumerate(chains_of(COUNT[AXES[part][stage]])):
            for step in range(steps):
                ring_copy(part, stage, chain, step).wait_send()

    def last_copy(part, offset):
        axis = AXES[part][2]
        n = COUNT[axis]
        return remote(
            stage3[part].at[(place[axis] + offset) % n], slots3[part].at[offset - 1],
            send3.at[part, offset - 1], recv3.at[part, offset - 1], moved(axis, offset),
        )

    def last_begin(part):
        for offset in range(1, COUNT[AXES[part][2]]):
            last_copy(part, offset).start()

    def all_copy(part, offset):
        mine = gathered.at[dp, pl.ds(FIRST_OF[part], TILES_OF[part])]
        return remote(
            mine, mine, all_send.at[part, offset - 1], all_recv.at[part, offset - 1],
            {"dp": (dp + offset) % 8, "graph": graph},
        )

    def last_end(part):
        axis = AXES[part][2]
        whole = stage3[part][place[axis]]
        for offset in range(1, COUNT[axis]):
            last_copy(part, offset).wait_recv()
            whole = whole + slots3[part][offset - 1]
        gathered[dp, pl.ds(FIRST_OF[part], TILES_OF[part])] = whole
        for offset in range(1, 8):
            all_copy(part, offset).start()

    def ready(had, have):
        for part in range(3):
            if had < 4 * (FIRST_OF[part] + TILES_OF[part]) <= have:
                begin(part, 0, (0, 1))

    def put(which, tile, row_y, v):
        at = PLACE[which][tile]
        part, px, pk = spot(at)
        if part == 0:
            part0[:, px, row_y, pk] = v
        elif part == 1:
            part1[px, row_y, :, pk] = v
        else:
            part2[row_y, px, :, pk] = v

    def pair(block, width):
        return jnp.concatenate([d_s[block + k] for k in range(width)], axis=1)

    def factor(block, count):
        return xt_s[pl.ds(block, count)].reshape(count * LANES, 2 * PADDED)

    def put_aligned(v, first_blocks):
        shaped = v.reshape(NZ, NY * 3, 8, v.shape[1])
        for w, b in enumerate(first_blocks):
            for row_y in range(NY):
                for i in range(3):
                    put(0, (1, i, b), row_y, shaped[:, row_y * 3 + i, :, w * LANES : (w + 1) * LANES])

    def put_shifted(which, matrix, tiles, shard, v, first_blocks):
        result[:, pl.ds(0, NY * shard), pl.ds(0, v.shape[1])] = v.reshape(NZ, NY * shard, v.shape[1])
        for w, b in enumerate(first_blocks):
            for row_y in range(NY):
                for i in range(tiles):
                    put(which, (matrix, i, b), row_y, result[:, pl.ds(row_y * shard + i * 8, 8), cols(w)])

    def two_blocks(which, at, width):
        dp_, dn_ = pair(AT_P2 + at, width), pair(AT_N2 + at, width)
        rp, rn = factor(AT_P2, TWO), factor(AT_N2, TWO)
        put_shifted(which, 2, 3, 20, dot(rp, dp_) + dot(rn, dn_), range(at, at + width))
        put_shifted(which, 2, 3, 20, dot(rp, dn_) - dot(rn, dp_), range(TWO + at, TWO + at + width))


    orders = ((0, AT_P1), (AT_P1, AT_P2), (AT_P2, BLOCKS))

    def halo_copies(k):
        span = pl.ds(orders[k][0] * LANES, (orders[k][1] - orders[k][0]) * LANES)
        return (
            remote(
                tab_ref.at[pl.ds(16, 16), span], tab_ref.at[pl.ds(32, 16), span],
                halo_send.at[k, 0], halo_recv.at[k, 0], after,
            ),
            remote(
                tab_ref.at[pl.ds(0, 16), span], tab_ref.at[pl.ds(48, 16), span],
                halo_send.at[k, 1], halo_recv.at[k, 1], before,
            ),
        )

    first_atom = graph * 16 - 8

    def table_row(atoms, shift):
        local = atoms - first_atom
        block = local >> 3
        base = jnp.where(block == 0, 32, jnp.where(block == 1, 0, jnp.where(block == 2, 16, 48)))
        return (base + (local & 7) + shift).astype(F32)

    row = lax.broadcasted_iota(jnp.int32, (8, EDGES), 0)
    phases = jnp.broadcast_to(angle_ref[...], (8, EDGES))
    phases = jnp.where(row < 2, phases, 2.0 * phases)
    ends = jnp.where(row == 4, table_row(source_ref[...], 0), table_row(target_ref[...], 8))
    rows = jnp.where(row >= 4, ends, jnp.where((row & 1) == 0, jnp.cos(phases), jnp.sin(phases)))
    parts = jnp.concatenate(list(split3(rows)), axis=0)
    pick_row = lax.broadcasted_iota(jnp.int32, (24, 6 * LANES), 0)
    pick_col = lax.broadcasted_iota(jnp.int32, (24, 6 * LANES), 1)
    chosen = jnp.where(pick_row % 8 == pick_col // LANES, 1.0, 0.0).astype(BF16)
    spread = dot_first(parts, chosen)
    for k in range(4):
        trig_s[k] = spread[:, k * LANES : (k + 1) * LANES]
    lane = lax.broadcasted_iota(jnp.int32, (EDGES, LANES), 1).astype(F32)
    for k in range(2):
        oh_s[k] = jnp.where(spread[:, (4 + k) * LANES : (5 + k) * LANES] == lane, 1.0, 0.0).astype(BF16)
    depth = tab_ref.shape[0]
    oh_src = oh_s[0, :, :depth]
    oh_dst = oh_s[1, :, :depth]

    pl.semaphore_wait(barrier, len(peers))

    for k in range(3):
        for copy in halo_copies(k):
            copy.start()
    xt_s[:, :, EDGES:PADDED] = jnp.zeros((BLOCKS, LANES, PADDED - EDGES), BF16)
    d_s[:, EDGES:PADDED, :] = jnp.zeros((BLOCKS, PADDED - EDGES, LANES), BF16)
    result[...] = jnp.zeros_like(result)

    def keep_x(block, width, v):
        x_s[:, cols(block, width)] = v
        for w in range(width):
            xt_s[block + w, :, :EDGES] = v[:, w * LANES : (w + 1) * LANES].T

    def rotated(onehot, c, s, plus, minus, width):
        a = dot(onehot, tab_ref[:, cols(plus, width)])
        b = dot(onehot, tab_ref[:, cols(minus, width)])
        return c * a - s * b, s * a + c * b

    for copy in halo_copies(0):
        copy.wait_recv()
    for at, width in chunks(ZERO):
        keep_x(at, width, dot(oh_src, tab_ref[:, cols(at, width)]).astype(BF16))
    for m, (count, plus, minus) in enumerate(((ONE, AT_P1, AT_N1), (TWO, AT_P2, AT_N2))):
        for copy in halo_copies(1 + m):
            copy.wait_recv()
        for at, width in chunks(count):
            c, s = wide(trig_s[2 * m], width), wide(trig_s[2 * m + 1], width)
            p, n = rotated(oh_src, c, s, plus + at, minus + at, width)
            keep_x(plus + at, width, p.astype(BF16))
            keep_x(minus + at, width, n.astype(BF16))


    def share(chosen):
        for other in range(2):
            spans = [k for k, span in enumerate(SHARES[other]) if chosen(*span)]
            if spans:
                @pl.when(core == 1 - other)
                def _(other=other, spans=spans):
                    for k in spans:
                        share_copy(k, SHARES[other][k]).start()

    share(lambda kind, lo, hi: kind == 0)
    for load in loads:
        load.wait()
    total = jnp.zeros((EDGES, LANES), F32)
    first = None
    for at, width in chunks(ZERO):
        out = dot(x_s[:, cols(0, ZERO)], w0_ref[:, cols(at, width)])
        if at == 0:
            first = out[:, :LANES]
        up = dot(oh_dst, tab_ref[:, cols(at, width)])
        du_s[:, cols(at, width)] = up
        total = total + folded(up * out, width)
    for m, (count, plus, minus, w_ref) in enumerate(((ONE, AT_P1, AT_N1, w1_ref), (TWO, AT_P2, AT_N2, w2_ref))):
        for at, width in chunks(count):
            c, s = wide(trig_s[2 * m], width), wide(trig_s[2 * m + 1], width)
            up_p, up_n = rotated(oh_dst, c, s, plus + at, minus + at, width)
            du_s[:, cols(plus + at, width)] = up_p
            du_s[:, cols(minus + at, width)] = up_n
            xp, xn = x_s[:, cols(plus, count)], x_s[:, cols(minus, count)]
            left, right = w_ref[:, cols(at, width)], w_ref[:, cols(count + at, width)]
            out_p = dot(xp, left) - dot(xn, right)
            out_n = dot(xp, right) + dot(xn, left)
            total = total + folded(up_p * out_p + up_n * out_n, width)

    size = LANES // HEADS
    head_r = lax.broadcasted_iota(jnp.int32, (LANES, LANES), 0) // size
    head_c = lax.broadcasted_iota(jnp.int32, (LANES, LANES), 1) // size
    same = jnp.where(head_r == head_c, 1.0, 0.0).astype(BF16)

    def head_sum(v):
        high, middle, low = split3(v)
        return dot(low, same) + dot(middle, same) + dot(high, same)

    scale = 1.0 / (float(size) ** 0.5)
    gate = jax.nn.sigmoid(head_sum(first) * scale)
    dlogit = head_sum(total) * gate * (1.0 - gate) * scale
    for block in MADE:
        v = du_s[:, cols(block)] * gate
        if block == 0:
            v = v + dlogit
        d_s[block, :EDGES, :] = v.astype(BF16)
        share(lambda kind, lo, hi: kind == 1 and block + 1 == hi)


    atoms = node_ref.shape[0]
    atom = lax.broadcasted_iota(jnp.int32, (atoms, EDGES), 0)
    table_row = jnp.where(atom < 8, atom + 32, jnp.where(atom < 16, atom - 8, jnp.where(atom < 24, atom, atom + 24)))
    oh_rows = jnp.where(table_row.astype(F32) == rows[4:5, :], 1.0, 0.0).astype(BF16)

    def scatter(block, width, v):
        high, low = split2(v)
        node_ref[:, cols(block, width)] = dot(oh_rows, high) + dot(oh_rows, low)

    def dconv(block, count):
        return jnp.concatenate([d_s[block + k, :EDGES, :] for k in range(count)], axis=1)

    def back(m, picked):
        count, plus, minus, w_ref = ((ONE, AT_P1, AT_N1, w1_ref), (TWO, AT_P2, AT_N2, w2_ref))[m]
        gp, gn = dconv(plus, count), dconv(minus, count)
        for at, width in chunks(count)[picked]:
            c, s = wide(trig_s[2 * m], width), wide(trig_s[2 * m + 1], width)
            left, right = w_ref[cols(at, width), cols(0, count)], w_ref[cols(at, width), cols(count, count)]
            back_p = dot_t(gp, left) + dot_t(gn, right)
            back_n = dot_t(gn, left) - dot_t(gp, right)
            scatter(plus + at, width, c * back_p + s * back_n)
            scatter(minus + at, width, c * back_n - s * back_p)


    def back_zero(picked):
        dz = dconv(AT_Z, ZERO)
        for at, width in chunks(ZERO)[picked]:
            scatter(at, width, dot_t(dz, w0_ref[cols(at, width), :]))

    @pl.when(core == 0)
    def _():
        share_copy(0, SHARES[0][0]).wait_recv()
        for j in range(3):
            for k in (1 + 2 * j, 2 + 2 * j):
                share_copy(k, SHARES[0][k]).wait_recv()
            dp_, dn_ = pair(AT_P1 + 2 * j, 2), pair(AT_N1 + 2 * j, 2)
            rp, rn = factor(AT_P1, ONE), factor(AT_N1, ONE)
            put_aligned(dot(rp, dp_) + dot(rn, dn_), (2 * j, 2 * j + 1))
            put_aligned(dot(rp, dn_) - dot(rn, dp_), (6 + 2 * j, 7 + 2 * j))
            ready(12 * j, 12 * j + 12)
        for k in (7, 8):
            share_copy(k, SHARES[0][k]).wait_recv()
        two_blocks(0, 0, 2)
        ready(36, 48)
        for k, span in enumerate(SHARES[1]):
            share_copy(k, span).wait_send()

    @pl.when(core == 1)
    def _():
        for k in (0, 2):
            share_copy(k, SHARES[1][k]).wait_recv()
        blank = jnp.zeros((NZ, 8, LANES), F32)
        for row_y in range(NY):
            for at in (46, 47):
                part2[row_y, spot(at)[1], :, spot(at)[2]] = blank
        for at, width in chunks(ZERO):
            put_shifted(1, 0, 4, 28, dot(factor(AT_Z, ZERO), pair(AT_Z + at, width)), range(at, at + width))
            ready(4 * at, 4 * (at + width))
        for k in (1, 3, 4):
            share_copy(k, SHARES[1][k]).wait_recv()
        two_blocks(1, 2, 2)
        two_blocks(1, 4, 1)
        ready(28, 48)
        for k, span in enumerate(SHARES[0]):
            share_copy(k, span).wait_send()

    begin(0, 0, (2, 3))
    advance(0, 0, 1, (0, 1))
    begin(1, 0, (2, 3))
    begin(2, 0, (2, 3))
    advance(0, 0, 1, (2, 3))
    back_zero(slice(0, 4))
    advance(1, 0, 1)
    advance(2, 0, 1)
    advance(0, 0, 2, (0, 1))
    advance(0, 0, 2, (2, 3))
    back(0, slice(0, 1))
    advance(0, 0, 3)
    back(0, slice(1, 2))
    finish(1, 0, s21)
    begin(1, 1)
    finish(0, 0, s20)
    begin(0, 1)
    finish(2, 0, s22)
    begin(2, 1)
    back(0, slice(2, 3))
    advance(1, 1, 1)
    advance(0, 1, 1)
    advance(2, 1, 1)
    back(1, slice(1, 2))
    finish(1, 1, s31)
    last_begin(1)
    finish(0, 1, s30)
    last_begin(0)
    back(1, slice(0, 1))
    finish(2, 1, s32)
    last_begin(2)
    back(1, slice(2, 3))
    node_up.start()
    node_down.start()
    last_end(0)
    last_end(1)
    last_end(2)
    node_up.wait()
    node_down.wait()
    nodes_out[pl.ds(0, 8)] = (node_ref[pl.ds(8, 8)] + node_in[0]).astype(BF16)
    nodes_out[pl.ds(8, 8)] = (node_ref[pl.ds(16, 8)] + node_in[1]).astype(BF16)
    for part in range(3):
        for stage in range(2):
            sent(part, stage)
        for offset in range(1, COUNT[AXES[part][2]]):
            last_copy(part, offset).wait_send()
    for part in range(3):
        for offset in range(1, 8):
            all_copy(part, offset).wait_recv()
    tiles_out[...] = gathered[...] * 0.125
    for part in range(3):
        for offset in range(1, 8):
            all_copy(part, offset).wait_send()
    for k in range(3):
        for copy in halo_copies(k):
            copy.wait_send()


def place_kernel(tiles_ref, nodes_ref, nodes_out, zero_out, one_out, two_out):
    nodes_out[...] = nodes_ref[...]
    outs = (zero_out, one_out, two_out)
    for which in range(2):
        for at, (matrix, i, b) in enumerate(TILES[which]):
            part, px, pk = spot(at)
            out = outs[matrix]
            rows = min(8, out.shape[0] - 8 * i)
            out[pl.ds(8 * i, rows), cols(b)] = tiles_ref[px * 2 + which, FIRST_OF[part] + pk, pl.ds(0, rows)]


def shards(node_feats, node_cotan, source, target, angle, w_zero, w_one, w_two):
    width = node_feats.shape[2]
    vmem = pl.BlockSpec(memory_space=pltpu.VMEM)
    hbm = pl.BlockSpec(memory_space=pl.ANY)
    dims = [[COUNT[a] for a in axes] for axes in AXES]
    tile = [(k, 8, LANES) for k in TILES_OF]

    def ring(part, stage):
        n = dims[part][stage]
        inner = dims[part][stage + 1 :]
        return pltpu.VMEM((2 * (n - 1), inner[0] // 2, *inner[1:], *tile[part]), F32)

    def leaf(part):
        pairs = dims[part][1] // 2 * dims[part][2] * TILES_OF[part] // 2
        return pltpu.VMEM((4, pairs, 16, LANES), BF16)

    dma = pltpu.SemaphoreType.DMA
    nodes, tiles = pl.pallas_call(
        edge_kernel,
        out_shape=(
            jax.ShapeDtypeStruct((16, width), BF16),
            jax.ShapeDtypeStruct((8, 12, 8, LANES), F32),
        ),
        in_specs=[vmem] * 5 + [hbm] * 3,
        out_specs=(vmem,) * 2,
        scratch_shapes=[
            pltpu.VMEM(w_zero.shape, BF16),
            pltpu.VMEM(w_one.shape, BF16),
            pltpu.VMEM(w_two.shape, BF16),
            pltpu.VMEM((64, width), BF16),
            pltpu.VMEM((EDGES, width), BF16),
            pltpu.VMEM((EDGES, width), F32),
            pltpu.VMEM((4, EDGES, LANES), F32),
            pltpu.VMEM((2, EDGES, LANES), BF16),
            pltpu.VMEM((32, width), F32),
            pltpu.VMEM((BLOCKS, LANES, 2 * PADDED), BF16),
            pltpu.VMEM((BLOCKS, 2 * PADDED, LANES), BF16),
            *[pltpu.VMEM((*dims[p], *tile[p]), F32) for p in range(3)],
            *[ring(p, 0) for p in range(3)],
            *[pltpu.VMEM((*dims[p][1:], *tile[p]), F32) for p in range(3)],
            *[ring(p, 1) for p in range(3)],
            *[pltpu.VMEM((dims[p][2], *tile[p]), F32) for p in range(3)],
            *[pltpu.VMEM((dims[p][2] - 1, *tile[p]), F32) for p in range(3)],
            *[leaf(p) for p in range(3)],
            *[leaf(p) for p in range(3)],
            pltpu.VMEM((8, 12, 8, LANES), F32),
            pltpu.VMEM((NZ, 120, 2 * LANES), F32),
            pltpu.VMEM((2, 8, width), F32),
            dma((3,)), dma((9,)), dma((9,)),
            dma((3, 14)), dma((3, 14)), dma((3, 14)), dma((3, 14)), dma((3, 7)), dma((3, 7)),
            dma((3, 7)), dma((3, 7)), dma((2,)), dma((2,)), dma((3, 2)), dma((3, 2)),
        ],
        compiler_params=pltpu.CompilerParams(
            vmem_limit_bytes=VMEM_LIMIT, collective_id=0, has_side_effects=True
        ),
        name="edge_gradients",
    )(node_feats[0], node_cotan[0], source, target, angle, w_zero, w_one, w_two)
    nodes, zero_g, one_g, two_g = pl.pallas_call(
        place_kernel,
        out_shape=(
            jax.ShapeDtypeStruct((16, width), BF16),
            jax.ShapeDtypeStruct((28, ZERO * LANES), F32),
            jax.ShapeDtypeStruct((24, 2 * ONE * LANES), F32),
            jax.ShapeDtypeStruct((20, 2 * TWO * LANES), F32),
        ),
        in_specs=[vmem] * 2,
        out_specs=(vmem,) * 4,
        name="place_tiles",
    )(tiles, nodes)
    return nodes[None], zero_g, one_g, two_g


def solution(mesh):
    placed = (
        P("dp", "graph", None),
        P("dp", "graph", None),
        P("dp", "graph"),
        P("dp", "graph"),
        P("dp", "graph"),
        P(),
        P(),
        P(),
    )
    return jax.shard_map(
        shards,
        mesh=mesh,
        in_specs=placed,
        out_specs=(P("dp", "graph", None), P("graph", None), P("graph", None), P("graph", None)),
        check_vma=False,
    )
```

```python
import jax
import jax.numpy as jnp
from jax import lax
from jax.experimental import pallas as pl
from jax.experimental.pallas import tpu as pltpu
from jax.sharding import PartitionSpec as P

MESH = pl.DeviceIdType.MESH
F32 = jnp.float32
BF16 = jnp.bfloat16
HEADS = 8
LANES = 128
EDGES = 320
PADDED = 384
BLOCKS = 29
ZERO, ONE, TWO = 7, 6, 5
AT_Z, AT_P1, AT_N1, AT_P2, AT_N2 = 0, 7, 13, 19, 24
VMEM_LIMIT = 62 * 1024 * 1024


def dot(a, b):
    return jnp.dot(a, b, preferred_element_type=F32)


def dot_t(a, b):
    return lax.dot_general(a, b, (((1,), (1,)), ((), ())), preferred_element_type=F32)


def dot_first(a, b):
    return lax.dot_general(a, b, (((0,), (0,)), ((), ())), preferred_element_type=F32)


def split2(v):
    high = v.astype(BF16)
    return high, (v - high.astype(F32)).astype(BF16)


def split3(v):
    high = v.astype(BF16)
    rest = v - high.astype(F32)
    middle = rest.astype(BF16)
    return high, middle, (rest - middle.astype(F32)).astype(BF16)


def chunks(count):
    out, at = [], 0
    while at < count:
        width = min(2, count - at)
        out.append((at, width))
        at += width
    return out


def cols(block, width=1):
    return pl.ds(block * LANES, width * LANES)


def wide(v, width):
    return v if width == 1 else jnp.concatenate([v] * width, axis=1)


def folded(v, width):
    return v if width == 1 else v[:, :LANES] + v[:, LANES:]


SHARES = (
    (
        (0, 7, 29), (1, 7, 9), (1, 13, 15), (1, 9, 11), (1, 15, 17), (1, 11, 13), (1, 17, 19),
        (1, 19, 21), (1, 24, 26),
    ),
    ((0, 0, 7), (0, 19, 29), (1, 0, 7), (1, 21, 24), (1, 26, 29)),
)
MADE = (
    7, 8, 13, 14, 0, 1, 2, 3, 4, 5, 6, 9, 10, 15, 16, 11, 12, 17, 18, 19, 20, 24, 25, 21, 22, 23, 26, 27, 28,
)
ONE_ORDER = tuple(b for j in range(3) for b in (2 * j, 2 * j + 1, 6 + 2 * j, 7 + 2 * j))
TILES = (
    tuple((1, i, b) for b in ONE_ORDER for i in range(3)) + tuple((2, i, b) for b in (0, 1, 5, 6) for i in range(3)),
    tuple((0, i, b) for b in range(7) for i in range(4)) + tuple((2, i, b) for b in (2, 3, 4, 7, 8, 9) for i in range(3)),
)
PLACE = tuple({tile: at for at, tile in enumerate(order)} for order in TILES)
NX, NY, NZ = 4, 4, 8
AXES = (("z", "x", "y"), ("x", "y", "z"), ("y", "x", "z"))
TILES_OF = (3, 4, 5)
FIRST_OF = (0, TILES_OF[0], TILES_OF[0] + TILES_OF[1])
COUNT = {"x": NX, "y": NY, "z": NZ}


def spot(at):
    part = 0 if at < 4 * FIRST_OF[1] else 1 if at < 4 * FIRST_OF[2] else 2
    inside = at - 4 * FIRST_OF[part]
    return part, inside // TILES_OF[part], inside % TILES_OF[part]


def chains_of(n):
    return ((1, 0, n // 2), (-1, 1, n // 2), (1, 1, n // 2 - 1), (-1, 0, n // 2 - 1))


def edge_kernel(
    feats_hbm, cotan_hbm, source_hbm, target_hbm, angle_hbm, w0_hbm, w1_hbm, w2_hbm,
    nodes_out, tiles_out,
    feats_ref, cotan_ref, source_ref, target_ref, angle_ref, w0_ref, w1_ref, w2_ref, tab_ref, x_s, du_s, trig_s, oh_s, node_ref,
    xt_s, d_s, part0, part1, part2, r10, r11, r12, s20, s21, s22, r20, r21, r22, s30, s31, s32, r30, r31, r32,
    o0, o1, o2, i0, i1, i2, gathered, result, node_in,
    load_sem, share_send, share_recv, send1, recv1, send2, recv2, send3, recv3, all_send, all_recv, node_send, node_recv,
    halo_send, halo_recv,
):
    dp = lax.axis_index("dp")
    graph = lax.axis_index("graph")
    core, x = dp % 2, dp // 2
    y, z = graph % NY, graph // NY
    place = {"x": x, "y": y, "z": z}

    def moved(axis, offset):
        n = COUNT[axis]
        to = (place[axis] + offset + n) % n
        if axis == "x":
            return {"dp": to * 2 + core, "graph": graph}
        if axis == "y":
            return {"dp": dp, "graph": z * NY + to}
        return {"dp": dp, "graph": to * NY + y}

    sibling = {"dp": x * 2 + (1 - core), "graph": graph}
    graphs = NY * NZ
    before = {"dp": dp, "graph": (graph + graphs - 1) % graphs}
    after = {"dp": dp, "graph": (graph + 1) % graphs}
    peers = [{"dp": (dp + o) % 8, "graph": graph} for o in range(1, 8)]
    peers += [moved("y", o) for o in range(1, NY)] + [moved("z", o) for o in range(1, NZ)] + [before, after]

    inputs = (
        (feats_hbm, feats_ref), (cotan_hbm, cotan_ref), (source_hbm, source_ref), (target_hbm, target_ref),
        (angle_hbm, angle_ref), (w0_hbm, w0_ref), (w1_hbm, w1_ref), (w2_hbm, w2_ref),
    )
    loads = [pltpu.make_async_copy(src, dst, load_sem.at[k]) for k, (src, dst) in enumerate(inputs)]
    for load in loads:
        load.start()
    barrier = pltpu.get_barrier_semaphore()
    for peer in peers:
        pl.semaphore_signal(barrier, inc=1, device_id=peer, device_id_type=MESH)
    for load in loads[:5]:
        load.wait()
    feats, cotan = feats_ref[...].astype(F32), cotan_ref[...].astype(F32)
    tab_ref[pl.ds(0, 16)] = jnp.concatenate([feats[:8], cotan[:8]], 0).astype(BF16)
    tab_ref[pl.ds(16, 16)] = jnp.concatenate([feats[8:], cotan[8:]], 0).astype(BF16)
    def remote(src, dst, send, recv, device):
        return pltpu.make_async_remote_copy(
            src_ref=src, dst_ref=dst, send_sem=send, recv_sem=recv, device_id=device, device_id_type=MESH
        )

    node_up = remote(node_ref.at[pl.ds(0, 8)], node_in.at[1], node_send.at[0], node_recv.at[0], before)
    node_down = remote(node_ref.at[pl.ds(24, 8)], node_in.at[0], node_send.at[1], node_recv.at[1], after)

    def own_half(kind, lo, hi, half):
        if kind == 0:
            return xt_s.at[pl.ds(lo, hi - lo), :, pl.ds(half * PADDED, PADDED)]
        return d_s.at[pl.ds(lo, hi - lo), pl.ds(half * PADDED, PADDED), :]

    def share_copy(k, span):
        return remote(own_half(*span, 0), own_half(*span, 1), share_send.at[k], share_recv.at[k], sibling)

    stage1 = (part0, part1, part2)
    rings1 = (r10, r11, r12)
    stage2 = (s20, s21, s22)
    rings2 = (r20, r21, r22)
    stage3 = (s30, s31, s32)
    slots3 = (r30, r31, r32)

    outs16, ins16 = (o0, o1, o2), (i0, i1, i2)

    def slot_of(n, chain, step):
        return sum(c[2] for c in chains_of(n)[:chain]) + step

    def ring_copy(part, stage, chain, step):
        axis = AXES[part][stage]
        n = COUNT[axis]
        way, half, steps = chains_of(n)[chain]
        source, ring = ((stage1, rings1), (stage2, rings2))[stage]
        sends, recvs = ((send1, recv1), (send2, recv2))[stage]
        deep = source[part].shape[1] // 2
        slot = slot_of(n, chain, step)
        if step == 0 and stage == 0:
            return remote(
                outs16[part].at[chain], ins16[part].at[chain],
                sends.at[part, slot], recvs.at[part, slot], moved(axis, way),
            )
        if step == 0:
            block = (place[axis] + way * steps + n) % n
            src = source[part].at[block, pl.ds(half * deep, deep)]
        else:
            src = ring[part].at[slot - 1]
        return remote(src, ring[part].at[slot], sends.at[part, slot], recvs.at[part, slot], moved(axis, way))

    def begin(part, stage, picked=(0, 1, 2, 3)):
        axis = AXES[part][stage]
        n = COUNT[axis]
        for chain in picked:
            way, half, steps = chains_of(n)[chain]
            if stage == 0:
                deep = stage1[part].shape[1] // 2
                block = (place[axis] + way * steps + n) % n
                v = stage1[part][block, pl.ds(half * deep, deep)]
                outs16[part][chain] = v.reshape(outs16[part].shape[1:]).astype(BF16)
            ring_copy(part, stage, chain, 0).start()

    def arrival(part, stage, chain, step):
        n = COUNT[AXES[part][stage]]
        ring = (rings1, rings2)[stage][part]
        if stage == 0 and step == 0:
            return ins16[part][chain].astype(F32).reshape(ring.shape[1:])
        return ring[slot_of(n, chain, step)]

    def advance(part, stage, step, picked=(0, 1, 2, 3)):
        axis = AXES[part][stage]
        n = COUNT[axis]
        source, ring = ((stage1, rings1), (stage2, rings2))[stage]
        deep = source[part].shape[1] // 2
        for chain, (way, half, steps) in enumerate(chains_of(n)):
            if step < steps and chain in picked:
                slot = slot_of(n, chain, step)
                ring_copy(part, stage, chain, step - 1).wait_recv()
                block = (place[axis] + way * (steps - step) + n) % n
                ring[part][slot - 1] = arrival(part, stage, chain, step - 1) + source[part][block, pl.ds(half * deep, deep)]
                ring_copy(part, stage, chain, step).start()

    def finish(part, stage, out):
        axis = AXES[part][stage]
        n = COUNT[axis]
        source, ring = ((stage1, rings1), (stage2, rings2))[stage]
        deep = source[part].shape[1] // 2
        for half in range(2):
            arrived = []
            for chain, (way, h, steps) in enumerate(chains_of(n)):
                if h == half:
                    ring_copy(part, stage, chain, steps - 1).wait_recv()
                    arrived.append(arrival(part, stage, chain, steps - 1))
            out[pl.ds(half * deep, deep)] = source[part][place[axis], pl.ds(half * deep, deep)] + arrived[0] + arrived[1]

    def sent(part, stage):
        for chain, (way, half, steps) in enumerate(chains_of(COUNT[AXES[part][stage]])):
            for step in range(steps):
                ring_copy(part, stage, chain, step).wait_send()

    def last_copy(part, offset):
        axis = AXES[part][2]
        n = COUNT[axis]
        return remote(
            stage3[part].at[(place[axis] + offset) % n], slots3[part].at[offset - 1],
            send3.at[part, offset - 1], recv3.at[part, offset - 1], moved(axis, offset),
        )

    def last_begin(part):
        for offset in range(1, COUNT[AXES[part][2]]):
            last_copy(part, offset).start()

    def all_copy(part, offset):
        mine = gathered.at[dp, pl.ds(FIRST_OF[part], TILES_OF[part])]
        return remote(
            mine, mine, all_send.at[part, offset - 1], all_recv.at[part, offset - 1],
            {"dp": (dp + offset) % 8, "graph": graph},
        )

    def last_end(part):
        axis = AXES[part][2]
        whole = stage3[part][place[axis]]
        for offset in range(1, COUNT[axis]):
            last_copy(part, offset).wait_recv()
            whole = whole + slots3[part][offset - 1]
        gathered[dp, pl.ds(FIRST_OF[part], TILES_OF[part])] = whole
        for offset in range(1, 8):
            all_copy(part, offset).start()

    def ready(had, have):
        for part in range(3):
            if had < 4 * (FIRST_OF[part] + TILES_OF[part]) <= have:
                begin(part, 0, (0, 1))

    def put(which, tile, row_y, v):
        at = PLACE[which][tile]
        part, px, pk = spot(at)
        if part == 0:
            part0[:, px, row_y, pk] = v
        elif part == 1:
            part1[px, row_y, :, pk] = v
        else:
            part2[row_y, px, :, pk] = v

    def pair(block, width):
        return jnp.concatenate([d_s[block + k] for k in range(width)], axis=1)

    def factor(block, count):
        return xt_s[pl.ds(block, count)].reshape(count * LANES, 2 * PADDED)

    def put_aligned(v, first_blocks):
        shaped = v.reshape(NZ, NY * 3, 8, v.shape[1])
        for w, b in enumerate(first_blocks):
            for row_y in range(NY):
                for i in range(3):
                    put(0, (1, i, b), row_y, shaped[:, row_y * 3 + i, :, w * LANES : (w + 1) * LANES])

    def put_shifted(which, matrix, tiles, shard, v, first_blocks):
        result[:, pl.ds(0, NY * shard), pl.ds(0, v.shape[1])] = v.reshape(NZ, NY * shard, v.shape[1])
        for w, b in enumerate(first_blocks):
            for row_y in range(NY):
                for i in range(tiles):
                    put(which, (matrix, i, b), row_y, result[:, pl.ds(row_y * shard + i * 8, 8), cols(w)])

    def two_blocks(which, at, width):
        dp_, dn_ = pair(AT_P2 + at, width), pair(AT_N2 + at, width)
        rp, rn = factor(AT_P2, TWO), factor(AT_N2, TWO)
        put_shifted(which, 2, 3, 20, dot(rp, dp_) + dot(rn, dn_), range(at, at + width))
        put_shifted(which, 2, 3, 20, dot(rp, dn_) - dot(rn, dp_), range(TWO + at, TWO + at + width))


    orders = ((0, AT_P1), (AT_P1, AT_P2), (AT_P2, BLOCKS))

    def halo_copies(k):
        span = pl.ds(orders[k][0] * LANES, (orders[k][1] - orders[k][0]) * LANES)
        return (
            remote(
                tab_ref.at[pl.ds(16, 16), span], tab_ref.at[pl.ds(32, 16), span],
                halo_send.at[k, 0], halo_recv.at[k, 0], after,
            ),
            remote(
                tab_ref.at[pl.ds(0, 16), span], tab_ref.at[pl.ds(48, 16), span],
                halo_send.at[k, 1], halo_recv.at[k, 1], before,
            ),
        )

    first_atom = graph * 16 - 8

    def table_row(atoms, shift):
        local = atoms - first_atom
        block = local >> 3
        base = jnp.where(block == 0, 32, jnp.where(block == 1, 0, jnp.where(block == 2, 16, 48)))
        return (base + (local & 7) + shift).astype(F32)

    row = lax.broadcasted_iota(jnp.int32, (8, EDGES), 0)
    phases = jnp.broadcast_to(angle_ref[...], (8, EDGES))
    phases = jnp.where(row < 2, phases, 2.0 * phases)
    ends = jnp.where(row == 4, table_row(source_ref[...], 0), table_row(target_ref[...], 8))
    rows = jnp.where(row >= 4, ends, jnp.where((row & 1) == 0, jnp.cos(phases), jnp.sin(phases)))
    parts = jnp.concatenate(list(split3(rows)), axis=0)
    pick_row = lax.broadcasted_iota(jnp.int32, (24, 6 * LANES), 0)
    pick_col = lax.broadcasted_iota(jnp.int32, (24, 6 * LANES), 1)
    chosen = jnp.where(pick_row % 8 == pick_col // LANES, 1.0, 0.0).astype(BF16)
    spread = dot_first(parts, chosen)
    for k in range(4):
        trig_s[k] = spread[:, k * LANES : (k + 1) * LANES]
    lane = lax.broadcasted_iota(jnp.int32, (EDGES, LANES), 1).astype(F32)
    for k in range(2):
        oh_s[k] = jnp.where(spread[:, (4 + k) * LANES : (5 + k) * LANES] == lane, 1.0, 0.0).astype(BF16)
    depth = tab_ref.shape[0]
    oh_src = oh_s[0, :, :depth]
    oh_dst = oh_s[1, :, :depth]

    pl.semaphore_wait(barrier, len(peers))

    for k in range(3):
        for copy in halo_copies(k):
            copy.start()
    xt_s[:, :, EDGES:PADDED] = jnp.zeros((BLOCKS, LANES, PADDED - EDGES), BF16)
    d_s[:, EDGES:PADDED, :] = jnp.zeros((BLOCKS, PADDED - EDGES, LANES), BF16)
    result[...] = jnp.zeros_like(result)

    def keep_x(block, width, v):
        x_s[:, cols(block, width)] = v
        for w in range(width):
            xt_s[block + w, :, :EDGES] = v[:, w * LANES : (w + 1) * LANES].T

    def rotated(onehot, c, s, plus, minus, width):
        a = dot(onehot, tab_ref[:, cols(plus, width)])
        b = dot(onehot, tab_ref[:, cols(minus, width)])
        return c * a - s * b, s * a + c * b

    for copy in halo_copies(0):
        copy.wait_recv()
    for at, width in chunks(ZERO):
        keep_x(at, width, dot(oh_src, tab_ref[:, cols(at, width)]).astype(BF16))
    for m, (count, plus, minus) in enumerate(((ONE, AT_P1, AT_N1), (TWO, AT_P2, AT_N2))):
        for copy in halo_copies(1 + m):
            copy.wait_recv()
        for at, width in chunks(count):
            c, s = wide(trig_s[2 * m], width), wide(trig_s[2 * m + 1], width)
            p, n = rotated(oh_src, c, s, plus + at, minus + at, width)
            keep_x(plus + at, width, p.astype(BF16))
            keep_x(minus + at, width, n.astype(BF16))


    def share(chosen):
        for other in range(2):
            spans = [k for k, span in enumerate(SHARES[other]) if chosen(*span)]
            if spans:
                @pl.when(core == 1 - other)
                def _(other=other, spans=spans):
                    for k in spans:
                        share_copy(k, SHARES[other][k]).start()

    share(lambda kind, lo, hi: kind == 0)
    for load in loads[5:]:
        load.wait()
    total = jnp.zeros((EDGES, LANES), F32)
    first = None
    for at, width in chunks(ZERO):
        out = dot(x_s[:, cols(0, ZERO)], w0_ref[:, cols(at, width)])
        if at == 0:
            first = out[:, :LANES]
        up = dot(oh_dst, tab_ref[:, cols(at, width)])
        du_s[:, cols(at, width)] = up
        total = total + folded(up * out, width)
    for m, (count, plus, minus, w_ref) in enumerate(((ONE, AT_P1, AT_N1, w1_ref), (TWO, AT_P2, AT_N2, w2_ref))):
        for at, width in chunks(count):
            c, s = wide(trig_s[2 * m], width), wide(trig_s[2 * m + 1], width)
            up_p, up_n = rotated(oh_dst, c, s, plus + at, minus + at, width)
            du_s[:, cols(plus + at, width)] = up_p
            du_s[:, cols(minus + at, width)] = up_n
            xp, xn = x_s[:, cols(plus, count)], x_s[:, cols(minus, count)]
            left, right = w_ref[:, cols(at, width)], w_ref[:, cols(count + at, width)]
            out_p = dot(xp, left) - dot(xn, right)
            out_n = dot(xp, right) + dot(xn, left)
            total = total + folded(up_p * out_p + up_n * out_n, width)

    size = LANES // HEADS
    head_r = lax.broadcasted_iota(jnp.int32, (LANES, LANES), 0) // size
    head_c = lax.broadcasted_iota(jnp.int32, (LANES, LANES), 1) // size
    same = jnp.where(head_r == head_c, 1.0, 0.0).astype(BF16)

    def head_sum(v):
        high, middle, low = split3(v)
        return dot(low, same) + dot(middle, same) + dot(high, same)

    scale = 1.0 / (float(size) ** 0.5)
    gate = jax.nn.sigmoid(head_sum(first) * scale)
    dlogit = head_sum(total) * gate * (1.0 - gate) * scale
    for block in MADE:
        v = du_s[:, cols(block)] * gate
        if block == 0:
            v = v + dlogit
        d_s[block, :EDGES, :] = v.astype(BF16)
        share(lambda kind, lo, hi: kind == 1 and block + 1 == hi)


    atoms = node_ref.shape[0]
    atom = lax.broadcasted_iota(jnp.int32, (atoms, EDGES), 0)
    table_row = jnp.where(atom < 8, atom + 32, jnp.where(atom < 16, atom - 8, jnp.where(atom < 24, atom, atom + 24)))
    oh_rows = jnp.where(table_row.astype(F32) == rows[4:5, :], 1.0, 0.0).astype(BF16)

    def scatter(block, width, v):
        high, low = split2(v)
        node_ref[:, cols(block, width)] = dot(oh_rows, high) + dot(oh_rows, low)

    def dconv(block, count):
        return jnp.concatenate([d_s[block + k, :EDGES, :] for k in range(count)], axis=1)

    def back(m, picked):
        count, plus, minus, w_ref = ((ONE, AT_P1, AT_N1, w1_ref), (TWO, AT_P2, AT_N2, w2_ref))[m]
        gp, gn = dconv(plus, count), dconv(minus, count)
        for at, width in chunks(count)[picked]:
            c, s = wide(trig_s[2 * m], width), wide(trig_s[2 * m + 1], width)
            left, right = w_ref[cols(at, width), cols(0, count)], w_ref[cols(at, width), cols(count, count)]
            back_p = dot_t(gp, left) + dot_t(gn, right)
            back_n = dot_t(gn, left) - dot_t(gp, right)
            scatter(plus + at, width, c * back_p + s * back_n)
            scatter(minus + at, width, c * back_n - s * back_p)


    def back_zero(picked):
        dz = dconv(AT_Z, ZERO)
        for at, width in chunks(ZERO)[picked]:
            scatter(at, width, dot_t(dz, w0_ref[cols(at, width), :]))

    @pl.when(core == 0)
    def _():
        share_copy(0, SHARES[0][0]).wait_recv()
        for j in range(3):
            for k in (1 + 2 * j, 2 + 2 * j):
                share_copy(k, SHARES[0][k]).wait_recv()
            dp_, dn_ = pair(AT_P1 + 2 * j, 2), pair(AT_N1 + 2 * j, 2)
            rp, rn = factor(AT_P1, ONE), factor(AT_N1, ONE)
            put_aligned(dot(rp, dp_) + dot(rn, dn_), (2 * j, 2 * j + 1))
            put_aligned(dot(rp, dn_) - dot(rn, dp_), (6 + 2 * j, 7 + 2 * j))
            ready(12 * j, 12 * j + 12)
        for k in (7, 8):
            share_copy(k, SHARES[0][k]).wait_recv()
        two_blocks(0, 0, 2)
        ready(36, 48)
        for k, span in enumerate(SHARES[1]):
            share_copy(k, span).wait_send()

    @pl.when(core == 1)
    def _():
        for k in (0, 2):
            share_copy(k, SHARES[1][k]).wait_recv()
        blank = jnp.zeros((NZ, 8, LANES), F32)
        for row_y in range(NY):
            for at in (46, 47):
                part2[row_y, spot(at)[1], :, spot(at)[2]] = blank
        for at, width in chunks(ZERO):
            put_shifted(1, 0, 4, 28, dot(factor(AT_Z, ZERO), pair(AT_Z + at, width)), range(at, at + width))
            ready(4 * at, 4 * (at + width))
        for k in (1, 3, 4):
            share_copy(k, SHARES[1][k]).wait_recv()
        two_blocks(1, 2, 2)
        two_blocks(1, 4, 1)
        ready(28, 48)
        for k, span in enumerate(SHARES[0]):
            share_copy(k, span).wait_send()

    begin(0, 0, (2, 3))
    advance(0, 0, 1, (0, 1))
    begin(1, 0, (2, 3))
    begin(2, 0, (2, 3))
    advance(0, 0, 1, (2, 3))
    back_zero(slice(0, 4))
    advance(1, 0, 1)
    advance(2, 0, 1)
    advance(0, 0, 2, (0, 1))
    advance(0, 0, 2, (2, 3))
    back(0, slice(0, 1))
    advance(0, 0, 3)
    back(0, slice(1, 2))
    finish(1, 0, s21)
    begin(1, 1)
    finish(0, 0, s20)
    begin(0, 1)
    finish(2, 0, s22)
    begin(2, 1)
    back(0, slice(2, 3))
    advance(1, 1, 1)
    advance(0, 1, 1)
    advance(2, 1, 1)
    back(1, slice(1, 2))
    finish(1, 1, s31)
    last_begin(1)
    finish(0, 1, s30)
    last_begin(0)
    back(1, slice(0, 1))
    finish(2, 1, s32)
    last_begin(2)
    back(1, slice(2, 3))
    node_up.start()
    node_down.start()
    last_end(0)
    last_end(1)
    last_end(2)
    node_up.wait()
    node_down.wait()
    nodes_out[pl.ds(0, 8)] = (node_ref[pl.ds(8, 8)] + node_in[0]).astype(BF16)
    nodes_out[pl.ds(8, 8)] = (node_ref[pl.ds(16, 8)] + node_in[1]).astype(BF16)
    for part in range(3):
        for stage in range(2):
            sent(part, stage)
        for offset in range(1, COUNT[AXES[part][2]]):
            last_copy(part, offset).wait_send()
    for part in range(3):
        for offset in range(1, 8):
            all_copy(part, offset).wait_recv()
    tiles_out[...] = gathered[...] * 0.125
    for part in range(3):
        for offset in range(1, 8):
            all_copy(part, offset).wait_send()
    for k in range(3):
        for copy in halo_copies(k):
            copy.wait_send()


def place_kernel(tiles_ref, nodes_ref, nodes_out, zero_out, one_out, two_out):
    nodes_out[...] = nodes_ref[...]
    outs = (zero_out, one_out, two_out)
    for which in range(2):
        for at, (matrix, i, b) in enumerate(TILES[which]):
            part, px, pk = spot(at)
            out = outs[matrix]
            rows = min(8, out.shape[0] - 8 * i)
            out[pl.ds(8 * i, rows), cols(b)] = tiles_ref[px * 2 + which, FIRST_OF[part] + pk, pl.ds(0, rows)]


def shards(node_feats, node_cotan, source, target, angle, w_zero, w_one, w_two):
    width = node_feats.shape[2]
    vmem = pl.BlockSpec(memory_space=pltpu.VMEM)
    hbm = pl.BlockSpec(memory_space=pl.ANY)
    dims = [[COUNT[a] for a in axes] for axes in AXES]
    tile = [(k, 8, LANES) for k in TILES_OF]

    def ring(part, stage):
        n = dims[part][stage]
        inner = dims[part][stage + 1 :]
        return pltpu.VMEM((2 * (n - 1), inner[0] // 2, *inner[1:], *tile[part]), F32)

    def leaf(part):
        pairs = dims[part][1] // 2 * dims[part][2] * TILES_OF[part] // 2
        return pltpu.VMEM((4, pairs, 16, LANES), BF16)

    dma = pltpu.SemaphoreType.DMA
    nodes, tiles = pl.pallas_call(
        edge_kernel,
        out_shape=(
            jax.ShapeDtypeStruct((16, width), BF16),
            jax.ShapeDtypeStruct((8, 12, 8, LANES), F32),
        ),
        in_specs=[hbm] * 8,
        out_specs=(vmem,) * 2,
        scratch_shapes=[
            pltpu.VMEM(node_feats.shape[1:], BF16),
            pltpu.VMEM(node_cotan.shape[1:], BF16),
            pltpu.VMEM(source.shape, jnp.int32),
            pltpu.VMEM(target.shape, jnp.int32),
            pltpu.VMEM(angle.shape, F32),
            pltpu.VMEM(w_zero.shape, BF16),
            pltpu.VMEM(w_one.shape, BF16),
            pltpu.VMEM(w_two.shape, BF16),
            pltpu.VMEM((64, width), BF16),
            pltpu.VMEM((EDGES, width), BF16),
            pltpu.VMEM((EDGES, width), F32),
            pltpu.VMEM((4, EDGES, LANES), F32),
            pltpu.VMEM((2, EDGES, LANES), BF16),
            pltpu.VMEM((32, width), F32),
            pltpu.VMEM((BLOCKS, LANES, 2 * PADDED), BF16),
            pltpu.VMEM((BLOCKS, 2 * PADDED, LANES), BF16),
            *[pltpu.VMEM((*dims[p], *tile[p]), F32) for p in range(3)],
            *[ring(p, 0) for p in range(3)],
            *[pltpu.VMEM((*dims[p][1:], *tile[p]), F32) for p in range(3)],
            *[ring(p, 1) for p in range(3)],
            *[pltpu.VMEM((dims[p][2], *tile[p]), F32) for p in range(3)],
            *[pltpu.VMEM((dims[p][2] - 1, *tile[p]), F32) for p in range(3)],
            *[leaf(p) for p in range(3)],
            *[leaf(p) for p in range(3)],
            pltpu.VMEM((8, 12, 8, LANES), F32),
            pltpu.VMEM((NZ, 120, 2 * LANES), F32),
            pltpu.VMEM((2, 8, width), F32),
            dma((8,)), dma((9,)), dma((9,)),
            dma((3, 14)), dma((3, 14)), dma((3, 14)), dma((3, 14)), dma((3, 7)), dma((3, 7)),
            dma((3, 7)), dma((3, 7)), dma((2,)), dma((2,)), dma((3, 2)), dma((3, 2)),
        ],
        compiler_params=pltpu.CompilerParams(
            vmem_limit_bytes=VMEM_LIMIT, collective_id=0, has_side_effects=True
        ),
        name="edge_gradients",
    )(node_feats[0], node_cotan[0], source, target, angle, w_zero, w_one, w_two)
    nodes, zero_g, one_g, two_g = pl.pallas_call(
        place_kernel,
        out_shape=(
            jax.ShapeDtypeStruct((16, width), BF16),
            jax.ShapeDtypeStruct((28, ZERO * LANES), F32),
            jax.ShapeDtypeStruct((24, 2 * ONE * LANES), F32),
            jax.ShapeDtypeStruct((20, 2 * TWO * LANES), F32),
        ),
        in_specs=[vmem] * 2,
        out_specs=(vmem,) * 4,
        name="place_tiles",
    )(tiles, nodes)
    return nodes[None], zero_g, one_g, two_g


def solution(mesh):
    placed = (
        P("dp", "graph", None),
        P("dp", "graph", None),
        P("dp", "graph"),
        P("dp", "graph"),
        P("dp", "graph"),
        P(),
        P(),
        P(),
    )
    return jax.shard_map(
        shards,
        mesh=mesh,
        in_specs=placed,
        out_specs=(P("dp", "graph", None), P("graph", None), P("graph", None), P("graph", None)),
        check_vma=False,
    )
```
